256 devices in a mesh: seg: 8 (over x, core), grp: 32 (over z, y).
Axes of the slice: x: 4, y: 4, z: 8, core: 2. Of those that a mesh axis runs over, the one named last changes fastest.
Arguments:
- feats: bfloat16 [262144, 256], P(('seg', 'grp')), may hold values from -6 to 6
- dest: int32 [262144], P(('seg', 'grp')), may hold values from 0 to 262143, as said below
- anchor: int32 [262144], P(('seg', 'grp')), may hold values from 0 to 262143, as said below
- ln_gain: float32 [256], replicated, may hold values from 0.5 to 1.5
- w_qkv: bfloat16 [256, 768], replicated
- w_out: bfloat16 [256, 256], replicated, may hold values from -0.375 to 0.375
- cotangent: bfloat16 [262144, 256], P(('seg', 'grp')), may hold values from -6 to 6
Outputs:
- out_feats: bfloat16 [262144, 256], P(('seg', 'grp'))
- grad_feats: bfloat16 [262144, 256], P(('seg', 'grp'))
- grad_qkv: float32 [256, 768], replicated
- grad_out: float32 [256, 256], replicated
- grad_gain: float32 [256], replicated
The draws below stay inside these ranges and needn't reach their ends.
Inputs may be any that keep to these rules, and one draw needn't show every extreme that they name: `dest`: A permutation. The owner of Hilbert position h is device h // 1024 (segment index times the group size plus group index). Of each device's cells exactly 64 are owned by the device of the next segment (cyclically) with the same group index, exactly 64 by that of the previous segment, and the others by devices of its own segment; at most 56 cells of one device are owned by any one device of its own segment, and that many for several pairs in every draw. `anchor`: the inverse permutation of dest.
All inputs are finite; a program needn't handle non-finite values.
Results may differ from the reference program's by a relative error of at most 0.015.
The reference program's roundings to bfloat16 on the way count: a program that leaves them out, or rounds other values in their place, can miss the bound.
Values may be sent and summed in bfloat16 or wider, within the bound.
No kernel may reach another device: no remote copies, remote signals or barrier semaphores. Data moves between devices by JAX's collectives and lax.ppermute only.
A program may use at most 64 MiB of HBM per device.

```python
import jax
import jax.numpy as jnp
import numpy as np
from jax import lax

D = 256
HEADS = 16
PATCH = 1024
CELL_DEV = 1024
CELLS = 262144
SPILL = 64
KEEP = 896
CAP = 56
N_SEG = 8
N_GRP = 32


def route_tables(key):
    cells = CELL_DEV
    groups = N_GRP
    segments = N_SEG
    devices = segments * groups
    spill = SPILL
    room = CAP
    busy = groups // 4
    rest = KEEP - busy * room
    quot = rest // (groups - busy)
    extra = rest - quot * (groups - busy)
    amounts = [room] * busy + [quot + 1] * extra + [quot] * (groups - busy - extra)
    ends = jnp.asarray(np.cumsum(np.array(amounts, dtype=np.int64)).astype(np.int32))
    key_rank, key_relabel, key_order = jax.random.split(key, 3)
    bits = jax.random.randint(key_rank, (devices, cells), 0, 2 ** 20, dtype=jnp.int32)
    score = bits * cells + jnp.arange(cells, dtype=jnp.int32)[None, :]
    ranks = jnp.argsort(jnp.argsort(score, axis=1), axis=1).astype(jnp.int32)
    tbits = jax.random.randint(key_relabel, (segments, groups), 0, 2 ** 20, dtype=jnp.int32)
    tscore = tbits * groups + jnp.arange(groups, dtype=jnp.int32)[None, :]
    tinverse = jnp.argsort(tscore, axis=1).astype(jnp.int32)
    labels = jnp.argsort(tinverse, axis=1).astype(jnp.int32)
    device = jnp.arange(devices, dtype=jnp.int32)[:, None]
    seg_of = device // groups
    grp_of = device % groups
    inner_product = ranks - 2 * spill
    bucket = jnp.sum((inner_product[:, :, None] >= ends[None, None, :]).astype(jnp.int32), axis=-1)
    bucket = jnp.minimum(bucket, groups - 1)
    target = (labels[seg_of, grp_of] + bucket) % groups
    peer = tinverse[seg_of, target]
    owner = jnp.where(ranks < spill, (seg_of + 1) % segments * groups + grp_of, jnp.where(ranks < 2 * spill, (seg_of + segments - 1) % segments * groups + grp_of, seg_of * groups + peer))
    flat_owner = owner.reshape(-1)
    shuffle = jax.random.permutation(key_order, CELLS).astype(jnp.int32)
    anchor = jnp.argsort(flat_owner * CELLS + shuffle).astype(jnp.int32)
    dest = jnp.zeros((CELLS,), jnp.int32).at[anchor].set(jnp.arange(CELLS, dtype=jnp.int32))
    return (dest, anchor)


def draw_dest(key, part):
    return route_tables(key)[0]


def draw_anchor(key, part):
    return route_tables(key)[1]


def draw_w_qkv(key, part):
    key = jax.random.fold_in(key, 7)
    whole = jax.random.normal(key, (D, 3 * D), jnp.float32) * D ** (-0.5)
    return whole.astype(jnp.bfloat16)


def steps_of(rng, shape, cuts, low, top_value):
    def one(dim, blocks):
        draws = jax.random.uniform(jax.random.fold_in(jax.random.fold_in(rng, 6), dim), (blocks,), jnp.float32, low / len(cuts), top_value / len(cuts))
        return jnp.repeat(jnp.exp(draws), shape[dim] // blocks).reshape((-1,) + (1,) * (len(shape) - dim - 1))

    gain = one(*cuts[0])
    for cut in cuts[1:]:
        gain = gain * one(*cut)
    return gain


def bell_draw(own_key, dims, scale, bound, cuts=(), kind=jnp.bfloat16):
    result = scale * jax.random.normal(own_key, dims, jnp.float32)
    if cuts:
        result = result * steps_of(own_key, dims, cuts, -0.22, 0.18)
    return jnp.clip(result, -bound, bound).astype(kind)


def setup_inputs(seed: int = 0) -> dict:
    key_list = jax.random.split(jax.random.key(seed), 8)
    return {
        "feats": bell_draw(key_list[0], (CELLS, D), 1.0, 6.0, ((0, 256),)),
        "dest": draw_dest(jax.random.fold_in(key_list[7], 71), 0),
        "anchor": draw_anchor(jax.random.fold_in(key_list[7], 71), 0),
        "ln_gain": jnp.clip(1.0 + 0.1 * jax.random.normal(key_list[3], (D,), jnp.float32), 0.5, 1.5),
        "w_qkv": draw_w_qkv(jax.random.fold_in(key_list[7], 71), 0),
        "w_out": bell_draw(key_list[5], (D, D), D ** -0.5, 0.375),
        "cotangent": bell_draw(key_list[6], (CELLS, D), 1.0, 6.0, ((0, 256),)),
    }


def split_heads(block, heads):
    rows, width = block.shape
    return block.reshape(rows, heads, width // heads).transpose(1, 0, 2)

def join_heads(block):
    heads, rows, size = block.shape
    return block.transpose(1, 0, 2).reshape(rows, heads * size)

def softmax_rows(query, keys, scale):
    scores = jnp.dot(query, keys.T, preferred_element_type=jnp.float32) * scale
    top = lax.optimization_barrier(jnp.max(scores, axis=-1, keepdims=True))
    expd = jnp.exp(scores - top)
    return expd / lax.optimization_barrier(jnp.sum(expd, axis=-1, keepdims=True))

def forward_patch(x, norm_gain, w_qkv, w_out):
    width = x.shape[1]
    scale = (width // HEADS) ** (-0.5)
    xf = x.astype(jnp.float32)
    centered_input = xf - lax.optimization_barrier(jnp.mean(xf, axis=-1, keepdims=True))
    inverse_deviation = lax.rsqrt(lax.optimization_barrier(jnp.mean(centered_input * centered_input, axis=-1, keepdims=True)) + 1e-05)
    standardized_input = centered_input * inverse_deviation
    normalized_input = (standardized_input * norm_gain).astype(jnp.bfloat16)
    query_key_value = jnp.dot(normalized_input, w_qkv, preferred_element_type=jnp.float32).astype(jnp.bfloat16)

    def one_head(parts):
        query, keys, values = parts
        probs = softmax_rows(query, keys, scale)
        return jnp.dot(probs.astype(jnp.bfloat16), values, preferred_element_type=jnp.float32).astype(jnp.bfloat16)
    heads_in = (split_heads(query_key_value[:, :width], HEADS), split_heads(query_key_value[:, width:2 * width], HEADS), split_heads(query_key_value[:, 2 * width:], HEADS))
    context_rows = join_heads(lax.map(one_head, heads_in))
    block_output = (xf + jnp.dot(context_rows, w_out, preferred_element_type=jnp.float32)).astype(jnp.bfloat16)
    return (block_output, (standardized_input, inverse_deviation, normalized_input, query_key_value, context_rows))

def backward_patch(g, saved_tensors, norm_gain, w_qkv, w_out):
    standardized_input, inverse_deviation, normalized_input, query_key_value, context_rows = saved_tensors
    width = g.shape[1]
    scale = (width // HEADS) ** (-0.5)
    grad_o = jnp.dot(context_rows.T, g, preferred_element_type=jnp.float32)
    d_ctx = jnp.dot(g, w_out.T, preferred_element_type=jnp.float32).astype(jnp.bfloat16)

    def one_head(parts):
        query, keys, values, dctx = parts
        probs = softmax_rows(query, keys, scale)
        probs_b = probs.astype(jnp.bfloat16)
        dprobs = jnp.dot(dctx, values.T, preferred_element_type=jnp.float32)
        dvalue = jnp.dot(probs_b.T, dctx, preferred_element_type=jnp.float32).astype(jnp.bfloat16)
        dscores = (probs * (dprobs - lax.optimization_barrier(jnp.sum(dprobs * probs, axis=-1, keepdims=True))) * scale).astype(jnp.bfloat16)
        dquery = jnp.dot(dscores, keys, preferred_element_type=jnp.float32).astype(jnp.bfloat16)
        dkey = jnp.dot(dscores.T, query, preferred_element_type=jnp.float32).astype(jnp.bfloat16)
        return (dquery, dkey, dvalue)
    heads_in = (split_heads(query_key_value[:, :width], HEADS), split_heads(query_key_value[:, width:2 * width], HEADS), split_heads(query_key_value[:, 2 * width:], HEADS), split_heads(d_ctx, HEADS))
    dquery, dkey, dvalue = lax.map(one_head, heads_in)
    d_qkv = jnp.concatenate([join_heads(dquery), join_heads(dkey), join_heads(dvalue)], axis=1)
    grad_q = jnp.dot(normalized_input.T, d_qkv, preferred_element_type=jnp.float32)
    normalized_gradient = jnp.dot(d_qkv, w_qkv.T, preferred_element_type=jnp.float32)
    gain_gradient = lax.optimization_barrier(jnp.sum(normalized_gradient * standardized_input, axis=0))
    standardized_gradient = normalized_gradient * norm_gain
    inner_product = standardized_gradient - lax.optimization_barrier(jnp.mean(standardized_gradient, axis=-1, keepdims=True)) - standardized_input * lax.optimization_barrier(jnp.mean(standardized_gradient * standardized_input, axis=-1, keepdims=True))
    dx = (g.astype(jnp.float32) + inner_product * inverse_deviation).astype(jnp.bfloat16)
    return (dx, grad_q, grad_o, gain_gradient)

def reference(feats, dest, anchor, ln_gain, w_qkv, w_out, cotangent):
    width = feats.shape[1]
    xh = feats[anchor]
    gh = cotangent[anchor]
    count = CELLS // PATCH

    def step(carry, pair):
        x, g = pair
        block_output, saved_tensors = forward_patch(x, ln_gain, w_qkv, w_out)
        dx, grad_q, grad_o, gain_gradient = backward_patch(g, saved_tensors, ln_gain, w_qkv, w_out)
        return ((carry[0] + grad_q, carry[1] + grad_o, carry[2] + gain_gradient), (block_output, dx))
    start = (jnp.zeros((width, 3 * width), jnp.float32), jnp.zeros((width, width), jnp.float32), jnp.zeros((width,), jnp.float32))
    sums, outs = lax.scan(step, start, (xh.reshape(count, PATCH, width), gh.reshape(count, PATCH, width)))
    yh = outs[0].reshape(CELLS, width)
    dxh = outs[1].reshape(CELLS, width)
    factor = CELLS ** (-0.5)
    return (yh[dest], dxh[dest], sums[0] * factor, sums[1] * factor, sums[2] * factor)
```

```python
import jax
import jax.numpy as jnp
from jax import lax
from jax.experimental import pallas as pl
from jax.experimental.pallas import tpu as pltpu
from jax.sharding import PartitionSpec as P

HEADS = 16
LANES = 128
PART = 256
f32 = jnp.float32
bf16 = jnp.bfloat16


def nn(a, b):
    return lax.dot_general(a, b, (((1,), (0,)), ((), ())), preferred_element_type=f32)


def nt(a, b):
    return lax.dot_general(a, b, (((1,), (1,)), ((), ())), preferred_element_type=f32)


def tn(a, b):
    return lax.dot_general(a, b, (((0,), (0,)), ((), ())), preferred_element_type=f32)


def column_of(row):
    return jnp.broadcast_to(row, (8, row.shape[1])).T[:, :1]


def one_hot(mark, like):
    return jnp.where(mark == like, 1.0, 0.0).astype(bf16)


def slots_of(value, seg, segments, groups, room, spill):
    cells = value.shape[1]
    owner = lax.div(value, cells)
    owner_seg = lax.div(owner, groups)
    owner_grp = owner - owner_seg * groups
    first = lax.rem(seg + 1, segments)
    inside = owner_seg == seg
    is_first = owner_seg == first
    bucket = jnp.where(inside, owner_grp, jnp.where(is_first, groups, groups + 1))
    flat = groups * room
    base = jnp.where(inside, owner_grp * room, jnp.where(is_first, flat, flat + spill))
    return bucket, base


def ranks_of(bucket, order):
    cells = bucket.shape[1]
    bucket_col = column_of(bucket.astype(f32))
    order_col = column_of(order.astype(f32))
    bucket_row = bucket.astype(f32)
    order_row = order.astype(f32)
    total = jnp.zeros((8, cells), f32)
    for start in range(0, cells, 8):
        same = bucket_col[start : start + 8] == bucket_row
        ahead = order_col[start : start + 8] < order_row
        total = total + jnp.where(same & ahead, 1.0, 0.0)
    return jnp.sum(total, axis=0, keepdims=True).astype(jnp.int32)


def picks(spots, rows, flat, tail):
    mine = spots[rows, :1]
    main = one_hot(lax.broadcasted_iota(jnp.int32, (LANES, flat), 1), mine)
    rest = one_hot(lax.broadcasted_iota(jnp.int32, (LANES, tail), 1) + flat, mine)
    return main, rest


def spread_slots(slot_row, spots):
    spots[...] = jnp.broadcast_to(
        column_of(slot_row[...].astype(f32)).astype(jnp.int32), spots.shape
    )


def pool_pick(slot_row, arrived, first, second, spots, target):
    spread_slots(slot_row, spots)
    edge = jnp.concatenate([first, second], axis=0)
    for start in range(0, target.shape[0], LANES):
        rows = slice(start, start + LANES)
        main, rest = picks(spots, rows, arrived.shape[0], edge.shape[0])
        target[rows, :] = (nn(main, arrived[...]) + nn(rest, edge)).astype(bf16)


def rows_at(slot_row, rows, start, count):
    spots = lax.broadcasted_iota(jnp.int32, (count, rows.shape[0]), 0) + start
    return nn(one_hot(spots, slot_row[...]), rows[...]).astype(bf16)


def pool_place(slot_row, rows, out):
    for start in range(0, out.shape[0], PART):
        out[start : start + PART, :] = rows_at(slot_row, rows, start, PART)


def plan_kernel(segments, groups, room, spill, seg_ref, dest, anchor, feats, cot, home, take, out, up, down):
    seg = seg_ref[0]
    cells, width = feats.shape
    flat = groups * room
    index = lax.broadcasted_iota(jnp.int32, (1, cells), 1)
    bucket, base = slots_of(dest[...], seg, segments, groups, room, spill)
    home[...] = base + ranks_of(bucket, index)
    source = anchor[...]
    bucket, base = slots_of(source, seg, segments, groups, room, spill)
    base = jnp.where(
        bucket == groups + 1, flat, jnp.where(bucket == groups, flat + spill, base)
    )
    take[...] = base + ranks_of(bucket, source)
    pool_place(home, feats, out)
    for rows, lanes in ((feats, slice(0, width)), (cot, slice(width, 2 * width))):
        tail = rows_at(home, rows, flat, 2 * spill)
        up[:, lanes] = tail[:spill]
        down[:, lanes] = tail[spill:]


def normalized(x, gain):
    xf = x.astype(f32)
    centered = xf - jnp.mean(xf, axis=-1, keepdims=True)
    rstd = lax.rsqrt(jnp.mean(centered * centered, axis=-1, keepdims=True) + 1e-05)
    xhat = centered * rstd
    return xhat, rstd, (xhat * gain).astype(bf16)


def attend(mode, first, count, k_all, v_all, refs, outs):
    q_t, k_t, v_t, d_t, q_zero, d_zero, score, expd, dprob, prob, dscore, stat, acc_v, acc_k = refs
    ctx_t, dq_t, dk_t, dv_t, lse = outs
    cells = score.shape[1]
    blocks = cells // PART
    size = q_t.shape[0] // HEADS
    backward = mode != "forward"
    forward = mode != "backward"
    last = first + count - 1
    TOP, SUM, INV, DOT, INNER = range(5)

    def rows(head):
        return pl.ds(pl.multiple_of(head * size, size), size)

    def rows8(head):
        return pl.ds(pl.multiple_of(head * 8, 8), 8)

    def part(index):
        return slice(index * PART, (index + 1) * PART)

    def fold(op, tile):
        return op(tile.reshape(PART // 8, 8, PART), axis=0)

    def combine(kind, block, piece, value, op):
        if piece:
            value = op(stat[kind, block % 2], value)
        stat[kind, block % 2] = value

    def spread(row):
        return jnp.broadcast_to(row, (8, PART))

    def set_head(head):
        slot = lax.rem(head, 2)
        old = rows(lax.rem(head + HEADS - 2, HEADS))
        new = rows(head)
        q_zero[slot, old, :] = jnp.zeros((size, cells), bf16)
        q_zero[slot, new, :] = q_t[new, :]
        if backward:
            d_zero[slot, old, :] = jnp.zeros((size, cells), bf16)
            d_zero[slot, new, :] = d_t[new, :]

    def stage_scores(head, block, piece):
        s = nn(k_all(part(piece)), q_zero[lax.rem(head, 2), :, part(block)])
        score[block % 2, part(piece), :] = s
        if forward:
            combine(TOP, block, piece, fold(jnp.max, s), jnp.maximum)
            if piece == blocks - 1:
                stat[TOP, block % 2] = spread(
                    jnp.max(stat[TOP, block % 2], axis=0, keepdims=True)
                )

    def stage_exp(head, block, piece):
        slot = block % 2
        top = stat[TOP, slot][:1] if forward else lse[rows8(head), part(block)][:1]
        e = jnp.exp(score[slot, part(piece), :] - top)
        expd[slot, part(piece), :] = e
        if forward:
            combine(SUM, block, piece, fold(jnp.sum, e), jnp.add)
        if backward:
            dp = nn(v_all(part(piece)), d_zero[lax.rem(head, 2), :, part(block)])
            dprob[slot, part(piece), :] = dp
            combine(DOT, block, piece, fold(jnp.sum, e * dp), jnp.add)
        if piece == blocks - 1:
            if forward:
                total = jnp.sum(stat[SUM, slot], axis=0, keepdims=True)
                inverse = 1.0 / total
                stat[INV, slot] = spread(inverse)
                if mode == "forward":
                    lse[rows8(head), part(block)] = spread(top + jnp.log(total))
            if backward:
                inner = jnp.sum(stat[DOT, slot], axis=0, keepdims=True)
                stat[INNER, slot] = spread(inner * inverse if forward else inner)

    def stage_probs(block, piece):
        slot = block % 2
        p = expd[slot, part(piece), :]
        if forward:
            p = p * stat[INV, slot][:1]
        prob[slot, part(piece), :] = p.astype(bf16)
        if backward:
            dp = dprob[slot, part(piece), :]
            dscore[slot, part(piece), :] = (p * (dp - stat[INNER, slot][:1])).astype(bf16)

    def stage_products(head, spot, block, piece):
        mine, out, slot, cols = rows(head), rows(spot), block % 2, part(block)
        if forward and piece == 0:
            ctx_t[out, cols] = nn(v_t[mine, :], prob[slot]).astype(bf16)
        if backward:
            if piece == 1:
                dq_t[out, cols] = nn(k_t[mine, :], dscore[slot]).astype(bf16)
            if piece == 2:
                more = nt(d_t[mine, cols], prob[slot])
                acc_v[...] = more if block == 0 else acc_v[...] + more
            if piece == 3:
                more = nt(q_t[mine, cols], dscore[slot])
                acc_k[...] = more if block == 0 else acc_k[...] + more
                if block == blocks - 1:
                    dv_t[out, :] = acc_v[...].astype(bf16)
                    dk_t[out, :] = acc_k[...].astype(bf16)

    def body(head, drain=False):
        before = lax.rem(head + HEADS - 1, HEADS)
        spot = jnp.where(head == first, HEADS, head - 1)
        for step in range(blocks - 1 if drain else blocks):
            for piece in range(blocks):
                late = step - 3
                if late < 0:
                    stage_products(before, spot, late + blocks, piece)
                elif not drain:
                    stage_products(head, head, late, piece)
                if not drain:
                    stage_scores(head, step, piece)
                late = step - 2
                if late < 0:
                    stage_probs(late + blocks, piece)
                elif not drain:
                    stage_probs(late, piece)
                late = step - 1
                if late < 0:
                    stage_exp(before, late + blocks, piece)
                elif not drain:
                    stage_exp(head, late, piece)

    def one_head(head, _):
        set_head(head)
        body(head)
        return 0

    q_zero[...] = jnp.zeros_like(q_zero)
    if backward:
        d_zero[...] = jnp.zeros_like(d_zero)
    lax.fori_loop(first, last + 1, one_head, 0)
    body(jnp.int32(last + 1), drain=True)


def forward_kernel(
    early, arrived, low, high, take, gain, w_qkv, w_t,
    xh, kv, q_t, k_t, v_t, ctx_t, lse,
    spots, *work,
):
    width = xh.shape[1]
    scale = (width // HEADS) ** -0.5
    pool_pick(take, arrived, low[:, :width], high[:, :width], spots, xh)
    _, _, normed = normalized(xh[...], gain[...])
    kv[...] = nn(normed, w_qkv[:, width:]).astype(bf16)
    q_t[...] = (nt(w_t[:width, :], normed).astype(bf16).astype(f32) * scale).astype(bf16)
    k_t[...] = (nt(w_t[width : 2 * width, :], normed).astype(bf16).astype(f32) * scale).astype(bf16)
    v_t[...] = nt(w_t[2 * width :, :], normed).astype(bf16)
    q_zero, score, expd, prob, stat = work
    refs = (q_t, k_t, v_t, None, q_zero, None, score, expd, None, prob, None, stat, None, None)
    attend(
        "forward", 0, early,
        lambda rows: kv[rows, :width], lambda rows: kv[rows, width:],
        refs, (ctx_t, None, None, None, lse),
    )


def middle_kernel(
    early, arrived, low, high, take, xh, kv, q_t, k_t, v_t, ctx_early, w_out,
    gh, d_t, dq_t, dk_t, dv_t, grad_out, back, back_low, back_high,
    spots, ctx_t, y, *work,
):
    cells, width = xh.shape
    spill = back_low.shape[0]
    done = early * (width // HEADS)
    pool_pick(take, arrived, low[:, width:], high[:, width:], spots, gh)
    d_t[...] = nt(w_out[...], gh[...]).astype(bf16)
    q_zero, d_zero, score, expd, dprob, prob, dscore, stat, acc_v, acc_k = work
    refs = (q_t, k_t, v_t, d_t, q_zero, d_zero, score, expd, dprob, prob, dscore, stat, acc_v, acc_k)
    attend(
        "both", early, HEADS - early,
        lambda rows: kv[rows, :width], lambda rows: kv[rows, width:],
        refs, (ctx_t, dq_t, dk_t, dv_t, None),
    )
    ctx_t[:done, :] = ctx_early[:done, :]
    grad_out[...] = nn(ctx_t[:width, :], gh[...])
    y[...] = (xh[...].astype(f32) + tn(ctx_t[:width, :], w_out[...])).astype(bf16)
    pool_place(take, y, back)
    tail = rows_at(take, y, back.shape[0], 2 * spill)
    back_low[...] = tail[:spill]
    back_high[...] = tail[spill:]


def backward_kernel(
    early, kv, q_t, k_t, v_t, d_t, lse, dq_late, dk_late, dv_late,
    d_qkv, dq_t, dk_t, dv_t, *work,
):
    width = q_t.shape[0]
    done = early * (width // HEADS)
    q_zero, d_zero, score, expd, dprob, prob, dscore, stat, acc_v, acc_k = work
    refs = (q_t, k_t, v_t, d_t, q_zero, d_zero, score, expd, dprob, prob, dscore, stat, acc_v, acc_k)
    attend(
        "backward", 0, early,
        lambda rows: kv[rows, :width], lambda rows: kv[rows, width:],
        refs, (None, dq_t, dk_t, dv_t, lse),
    )
    for i, (new, late) in enumerate(((dq_t, dq_late), (dk_t, dk_late), (dv_t, dv_late))):
        d_qkv[i * width : i * width + done, :] = new[:done, :]
        d_qkv[i * width + done : (i + 1) * width, :] = late[done:width, :]


def close_kernel(
    core, take, xh, gh, d_qkv, grad_out, y_low, y_high, gain, w_t,
    back, back_low, back_high, keep, give,
    dx, sums,
):
    cells, width = xh.shape
    spill = back_low.shape[0]
    xhat, rstd, normed = normalized(xh[...], gain[...])
    dn = tn(d_qkv[...], w_t[...])
    part_gain = jnp.sum(dn * xhat, axis=0, keepdims=True)
    sums[:, : 3 * width] = nn(d_qkv[...], normed).T
    sums[:, 3 * width : 4 * width] = grad_out[...]
    sums[:, 4 * width :] = jnp.broadcast_to(part_gain, (LANES, width)).T
    half = width // 2
    mine = core[0]
    keep[...] = sums[pl.ds(pl.multiple_of(mine * half, half), half), :]
    give[...] = sums[pl.ds(pl.multiple_of((1 - mine) * half, half), half), :]
    dxhat = dn * gain[...]
    inner = (
        dxhat
        - jnp.mean(dxhat, axis=-1, keepdims=True)
        - xhat * jnp.mean(dxhat * xhat, axis=-1, keepdims=True)
    )
    dx[...] = (gh[...].astype(f32) + inner * rstd).astype(bf16)
    pool_place(take, dx, back)
    tail = rows_at(take, dx, back.shape[0], 2 * spill)
    back_low[:, :width] = y_low[...]
    back_high[:, :width] = y_high[...]
    back_low[:, width:] = tail[:spill]
    back_high[:, width:] = tail[spill:]


def home_kernel(slot, y_arrived, dx_arrived, first, second, out, grad, spots):
    width = out.shape[1]
    spread_slots(slot, spots)
    edge = jnp.concatenate([first[...], second[...]], axis=0)
    for start in range(0, out.shape[0], LANES):
        rows = slice(start, start + LANES)
        main, rest = picks(spots, rows, y_arrived.shape[0], edge.shape[0])
        tail = nn(rest, edge)
        out[rows, :] = (nn(main, y_arrived[...]) + tail[:, :width]).astype(bf16)
        grad[rows, :] = (nn(main, dx_arrived[...]) + tail[:, width:]).astype(bf16)


def send_kernel(slot, rows, out):
    pool_place(slot, rows, out)


def finish_kernel(core, mine, other, grad_qkv, grad_out, grad_gain, total):
    width = grad_out.shape[1]
    half = mine.shape[0]
    total[pl.ds(pl.multiple_of(core[0] * half, half), half), :] = mine[...]
    total[pl.ds(pl.multiple_of((1 - core[0]) * half, half), half), :] = other[...]
    grad_qkv[...] = total[:, : 3 * width]
    grad_out[...] = total[:, 3 * width : 4 * width]
    grad_gain[...] = total[:, 4 * width :].T[:1, :]


def permuted(value, axis, target):
    count = lax.axis_size(axis)
    return lax.ppermute(value, axis, [(s, target(s) % count) for s in range(count)])


def all_to_all(value, axis, groups=None):
    return lax.all_to_all(
        value, axis, split_axis=0, concat_axis=0, tiled=True, axis_index_groups=groups
    )


def call(body, outs, scratch, args, flops, name, smem=False):
    shapes = [jax.ShapeDtypeStruct(s, d) for s, d in outs]
    return pl.pallas_call(
        body,
        out_shape=shapes,
        in_specs=[
            pl.BlockSpec(memory_space=pltpu.SMEM if smem and i == 0 else pltpu.VMEM)
            for i in range(len(args))
        ],
        out_specs=[pl.BlockSpec(memory_space=pltpu.VMEM)] * len(shapes),
        scratch_shapes=[pltpu.VMEM(s, d) for s, d in scratch],
        compiler_params=pltpu.CompilerParams(vmem_limit_bytes=58 * 2**20),
        cost_estimate=pl.CostEstimate(flops=flops, bytes_accessed=2**21, transcendentals=0),
        name=name,
    )(*args)


def after(value, *others):
    return lax.optimization_barrier((value, *others))[0]


def on_device(feats, dest, anchor, ln_gain, w_qkv, w_out, cotangent):
    cells, width = feats.shape
    groups = lax.axis_size("grp")
    segments = lax.axis_size("seg")
    spill = cells // 16
    room = 2 * (cells - 2 * spill) // groups
    flat = groups * room
    early = 8
    row_i = ((1, cells), jnp.int32)
    rows_b = ((cells, width), bf16)
    turned = ((width, cells), bf16)
    heads_t = ((width + width // HEADS, cells), bf16)
    leg = ((flat, width), bf16)
    edge = ((spill, width), bf16)
    edges = ((spill, 2 * width), bf16)
    spots = ((cells, LANES), jnp.int32)
    zeroed = ((2, width, cells), bf16)
    tile_f = ((2, cells, PART), f32)
    tile_b = ((2, cells, PART), bf16)
    stat = ((5, 2, 8, PART), f32)
    acc = ((width // HEADS, cells), f32)
    work = [zeroed, zeroed, tile_f, tile_f, tile_f, tile_b, tile_b, stat, acc, acc]
    seg = lax.axis_index("seg").astype(jnp.int32)
    core = (seg % 2).reshape(1)
    gain = ln_gain.reshape(1, width)
    w_t = w_qkv.T

    def exchange(rows):
        return all_to_all(rows.reshape(groups, room, width), "grp").reshape(flat, width)

    home, take, x_out, up, down = call(
        lambda *refs: plan_kernel(segments, groups, room, spill, *refs),
        [row_i, row_i, leg, edges, edges], [],
        (seg.reshape(1), dest.reshape(1, cells), anchor.reshape(1, cells), feats, cotangent),
        2**32, "plan", smem=True,
    )
    x_in = exchange(x_out)
    low = permuted(up, "seg", lambda s: s + 1)
    high = permuted(down, "seg", lambda s: s - 1)
    (g_out,) = call(send_kernel, [leg], [], (home, cotangent), 2**32, "send")
    g_in = exchange(after(g_out, x_in, low, high))
    xh, kv, q_t, k_t, v_t, ctx_t, lse = call(
        lambda *refs: forward_kernel(early, *refs),
        [rows_b, ((cells, 2 * width), bf16), turned, turned, turned, heads_t, ((HEADS * 8, cells), f32)],
        [spots, zeroed, tile_f, tile_f, tile_b, stat],
        (x_in, low, high, take, gain, w_qkv, w_t), 2**34, "forward",
    )
    gh, d_t, dq_t, dk_t, dv_t, grad_out, y_out, y_low, y_high = call(
        lambda *refs: middle_kernel(early, *refs),
        [rows_b, turned, heads_t, heads_t, heads_t, ((width, width), f32), leg, edge, edge],
        [spots, heads_t, rows_b, *work],
        (g_in, low, high, take, xh, kv, q_t, k_t, v_t, ctx_t, w_out), 2**35, "middle",
    )
    y_in = exchange(y_out)
    half = width // 2
    wide = 4 * width + LANES
    halves = ((half, wide), f32)
    (d_qkv,) = call(
        lambda *refs: backward_kernel(early, *refs),
        [((3 * width, cells), bf16)],
        [heads_t, heads_t, heads_t, *work],
        (kv, q_t, k_t, v_t, d_t, lse, dq_t, dk_t, dv_t), 2**35, "backward",
    )
    d_out, d_low, d_high, keep, give = call(
        close_kernel,
        [leg, edges, edges, halves, halves],
        [rows_b, ((width, wide), f32)],
        (core, take, xh, gh, after(d_qkv, y_in), grad_out, y_low, y_high, gain, w_t),
        2**32, "close", smem=True,
    )
    d_in = exchange(d_out)
    above = permuted(d_low, "seg", lambda s: s - 1)
    below = permuted(d_high, "seg", lambda s: s + 1)

    other = lambda s: s + 1 - 2 * (s % 2)
    rings = [list(range(c, segments, 2)) for c in range(2)]
    count = segments // 2
    share = half // count
    mine = keep + permuted(give, "seg", other)
    mine = jnp.sum(all_to_all(mine.reshape(count, share, wide), "seg", rings), axis=0)
    pieces = mine.reshape(groups, share // groups, wide)
    piece = jnp.sum(all_to_all(pieces, "grp"), axis=0) * (cells * segments * groups) ** -0.5
    piece = after(piece, d_in)
    mine = all_to_all(jnp.broadcast_to(piece[None], pieces.shape), "grp").reshape(1, share, wide)
    mine = all_to_all(jnp.broadcast_to(mine, (count, share, wide)), "seg", rings).reshape(half, wide)
    theirs = permuted(mine, "seg", other)
    out_feats, grad_feats = call(
        home_kernel, [rows_b, rows_b], [spots], (home, y_in, d_in, above, below), 2**32, "home"
    )
    grad_qkv, grad_out, grad_gain = call(
        finish_kernel,
        [((width, 3 * width), f32), ((width, width), f32), ((1, width), f32)],
        [((width, wide), f32)], (core, mine, theirs), 2**24, "finish", smem=True,
    )
    return out_feats, grad_feats, grad_qkv, grad_out, grad_gain.reshape(width)


def solution(mesh):
    split = P(("seg", "grp"), None)
    line = P(("seg", "grp"))
    return jax.shard_map(
        on_device,
        mesh=mesh,
        in_specs=(split, line, line, P(), P(), P(), split),
        out_specs=(split, split, P(), P(), P()),
        check_vma=False,
    )
```

```python
import jax
import jax.numpy as jnp
from jax import lax
from jax.experimental import pallas as pl
from jax.experimental.pallas import tpu as pltpu
from jax.sharding import PartitionSpec as P

HEADS = 16
LANES = 128
PART = 256
f32 = jnp.float32
bf16 = jnp.bfloat16


def nn(a, b):
    return lax.dot_general(a, b, (((1,), (0,)), ((), ())), preferred_element_type=f32)


def nt(a, b):
    return lax.dot_general(a, b, (((1,), (1,)), ((), ())), preferred_element_type=f32)


def tn(a, b):
    return lax.dot_general(a, b, (((0,), (0,)), ((), ())), preferred_element_type=f32)


def column_of(row):
    return jnp.broadcast_to(row, (8, row.shape[1])).T[:, :1]


def one_hot(mark, like):
    return jnp.where(mark == like, 1.0, 0.0).astype(bf16)


def slots_of(value, seg, segments, groups, room, spill):
    cells = value.shape[1]
    owner = lax.div(value, cells)
    owner_seg = lax.div(owner, groups)
    owner_grp = owner - owner_seg * groups
    first = lax.rem(seg + 1, segments)
    inside = owner_seg == seg
    is_first = owner_seg == first
    bucket = jnp.where(inside, owner_grp, jnp.where(is_first, groups, groups + 1))
    flat = groups * room
    base = jnp.where(inside, owner_grp * room, jnp.where(is_first, flat, flat + spill))
    return bucket, base


def ranks_of(bucket, order):
    cells = bucket.shape[1]
    bucket_col = column_of(bucket.astype(f32))
    order_col = column_of(order.astype(f32))
    bucket_row = bucket.astype(f32)
    order_row = order.astype(f32)
    total = jnp.zeros((8, cells), f32)
    for start in range(0, cells, 8):
        same = bucket_col[start : start + 8] == bucket_row
        ahead = order_col[start : start + 8] < order_row
        total = total + jnp.where(same & ahead, 1.0, 0.0)
    return jnp.sum(total, axis=0, keepdims=True).astype(jnp.int32)


def picks(spots, rows, flat, tail):
    mine = spots[rows, :1]
    main = one_hot(lax.broadcasted_iota(jnp.int32, (LANES, flat), 1), mine)
    rest = one_hot(lax.broadcasted_iota(jnp.int32, (LANES, tail), 1) + flat, mine)
    return main, rest


def spread_slots(slot_row, spots):
    spots[...] = jnp.broadcast_to(
        column_of(slot_row[...].astype(f32)).astype(jnp.int32), spots.shape
    )


def pool_pick(slot_row, arrived, first, second, spots, target):
    spread_slots(slot_row, spots)
    edge = jnp.concatenate([first, second], axis=0)
    for start in range(0, target.shape[0], LANES):
        rows = slice(start, start + LANES)
        main, rest = picks(spots, rows, arrived.shape[0], edge.shape[0])
        target[rows, :] = (nn(main, arrived[...]) + nn(rest, edge)).astype(bf16)


def rows_at(slot_row, rows, start, count):
    spots = lax.broadcasted_iota(jnp.int32, (count, rows.shape[0]), 0) + start
    return nn(one_hot(spots, slot_row[...]), rows[...]).astype(bf16)


def pool_place(slot_row, rows, out):
    for start in range(0, out.shape[0], PART):
        out[start : start + PART, :] = rows_at(slot_row, rows, start, PART)


def plan_kernel(segments, groups, room, spill, seg_ref, dest, feats, home, out):
    index = lax.broadcasted_iota(jnp.int32, dest.shape, 1)
    bucket, base = slots_of(dest[...], seg_ref[0], segments, groups, room, spill)
    home[...] = base + ranks_of(bucket, index)
    pool_place(home, feats, out)


def send_kernel(segments, groups, room, spill, seg_ref, anchor, home, feats, cot, take, out, up, down):
    width = feats.shape[1]
    flat = groups * room
    for rows, lanes in ((feats, slice(0, width)), (cot, slice(width, 2 * width))):
        tail = rows_at(home, rows, flat, 2 * spill)
        up[:, lanes] = tail[:spill]
        down[:, lanes] = tail[spill:]
    source = anchor[...]
    bucket, base = slots_of(source, seg_ref[0], segments, groups, room, spill)
    base = jnp.where(
        bucket == groups + 1, flat, jnp.where(bucket == groups, flat + spill, base)
    )
    take[...] = base + ranks_of(bucket, source)
    pool_place(home, cot, out)


def normalized(x, gain):
    xf = x.astype(f32)
    centered = xf - jnp.mean(xf, axis=-1, keepdims=True)
    rstd = lax.rsqrt(jnp.mean(centered * centered, axis=-1, keepdims=True) + 1e-05)
    xhat = centered * rstd
    return xhat, rstd, (xhat * gain).astype(bf16)


def attend(mode, first, count, k_all, v_all, refs, outs):
    q_t, k_t, v_t, d_t, q_zero, d_zero, score, expd, dprob, prob, dscore, stat, acc_v, acc_k = refs
    ctx_t, dq_t, dk_t, dv_t, lse = outs
    cells = score.shape[1]
    blocks = cells // PART
    size = q_t.shape[0] // HEADS
    backward = mode != "forward"
    forward = mode != "backward"
    last = first + count - 1
    TOP, SUM, INV, DOT, INNER = range(5)

    def rows(head):
        return pl.ds(pl.multiple_of(head * size, size), size)

    def rows8(head):
        return pl.ds(pl.multiple_of(head * 8, 8), 8)

    def part(index):
        return slice(index * PART, (index + 1) * PART)

    def fold(op, tile):
        return op(tile.reshape(PART // 8, 8, PART), axis=0)

    def combine(kind, block, piece, value, op):
        if piece:
            value = op(stat[kind, block % 2], value)
        stat[kind, block % 2] = value

    def spread(row):
        return jnp.broadcast_to(row, (8, PART))

    def set_head(head):
        slot = lax.rem(head, 2)
        old = rows(lax.rem(head + HEADS - 2, HEADS))
        new = rows(head)
        q_zero[slot, old, :] = jnp.zeros((size, cells), bf16)
        q_zero[slot, new, :] = q_t[new, :]
        if backward:
            d_zero[slot, old, :] = jnp.zeros((size, cells), bf16)
            d_zero[slot, new, :] = d_t[new, :]

    def stage_scores(head, block, piece):
        s = nn(k_all(part(piece)), q_zero[lax.rem(head, 2), :, part(block)])
        score[block % 2, part(piece), :] = s
        if forward:
            combine(TOP, block, piece, fold(jnp.max, s), jnp.maximum)
            if piece == blocks - 1:
                stat[TOP, block % 2] = spread(
                    jnp.max(stat[TOP, block % 2], axis=0, keepdims=True)
                )

    def stage_exp(head, block, piece):
        slot = block % 2
        top = stat[TOP, slot][:1] if forward else lse[rows8(head), part(block)][:1]
        e = jnp.exp(score[slot, part(piece), :] - top)
        expd[slot, part(piece), :] = e
        if forward:
            combine(SUM, block, piece, fold(jnp.sum, e), jnp.add)
        if backward:
            dp = nn(v_all(part(piece)), d_zero[lax.rem(head, 2), :, part(block)])
            dprob[slot, part(piece), :] = dp
            combine(DOT, block, piece, fold(jnp.sum, e * dp), jnp.add)
        if piece == blocks - 1:
            if forward:
                total = jnp.sum(stat[SUM, slot], axis=0, keepdims=True)
                inverse = 1.0 / total
                stat[INV, slot] = spread(inverse)
                if mode == "forward":
                    lse[rows8(head), part(block)] = spread(top + jnp.log(total))
            if backward:
                inner = jnp.sum(stat[DOT, slot], axis=0, keepdims=True)
                stat[INNER, slot] = spread(inner * inverse if forward else inner)

    def stage_probs(block, piece):
        slot = block % 2
        p = expd[slot, part(piece), :]
        if forward:
            p = p * stat[INV, slot][:1]
        prob[slot, part(piece), :] = p.astype(bf16)
        if backward:
            dp = dprob[slot, part(piece), :]
            dscore[slot, part(piece), :] = (p * (dp - stat[INNER, slot][:1])).astype(bf16)

    def stage_products(head, spot, block, piece):
        mine, out, slot, cols = rows(head), rows(spot), block % 2, part(block)
        if forward and piece == 0:
            ctx_t[out, cols] = nn(v_t[mine, :], prob[slot]).astype(bf16)
        if backward:
            if piece == 1:
                dq_t[out, cols] = nn(k_t[mine, :], dscore[slot]).astype(bf16)
            if piece == 2:
                more = nt(d_t[mine, cols], prob[slot])
                acc_v[...] = more if block == 0 else acc_v[...] + more
            if piece == 3:
                more = nt(q_t[mine, cols], dscore[slot])
                acc_k[...] = more if block == 0 else acc_k[...] + more
                if block == blocks - 1:
                    dv_t[out, :] = acc_v[...].astype(bf16)
                    dk_t[out, :] = acc_k[...].astype(bf16)

    def body(head, drain=False):
        before = lax.rem(head + HEADS - 1, HEADS)
        spot = jnp.where(head == first, HEADS, head - 1)
        for step in range(blocks - 1 if drain else blocks):
            for piece in range(blocks):
                late = step - 3
                if late < 0:
                    stage_products(before, spot, late + blocks, piece)
                elif not drain:
                    stage_products(head, head, late, piece)
                if not drain:
                    stage_scores(head, step, piece)
                late = step - 2
                if late < 0:
                    stage_probs(late + blocks, piece)
                elif not drain:
                    stage_probs(late, piece)
                late = step - 1
                if late < 0:
                    stage_exp(before, late + blocks, piece)
                elif not drain:
                    stage_exp(head, late, piece)

    def one_head(head, _):
        set_head(head)
        body(head)
        return 0

    q_zero[...] = jnp.zeros_like(q_zero)
    if backward:
        d_zero[...] = jnp.zeros_like(d_zero)
    lax.fori_loop(first, last + 1, one_head, 0)
    body(jnp.int32(last + 1), drain=True)


def forward_kernel(
    early, arrived, low, high, take, gain, w_qkv, w_t,
    xh, kv, q_t, k_t, v_t, ctx_t, lse,
    spots, *work,
):
    width = xh.shape[1]
    scale = (width // HEADS) ** -0.5
    pool_pick(take, arrived, low[:, :width], high[:, :width], spots, xh)
    _, _, normed = normalized(xh[...], gain[...])
    kv[...] = nn(normed, w_qkv[:, width:]).astype(bf16)
    q_t[...] = (nt(w_t[:width, :], normed).astype(bf16).astype(f32) * scale).astype(bf16)
    k_t[...] = (nt(w_t[width : 2 * width, :], normed).astype(bf16).astype(f32) * scale).astype(bf16)
    v_t[...] = nt(w_t[2 * width :, :], normed).astype(bf16)
    q_zero, score, expd, prob, stat = work
    refs = (q_t, k_t, v_t, None, q_zero, None, score, expd, None, prob, None, stat, None, None)
    attend(
        "forward", 0, early,
        lambda rows: kv[rows, :width], lambda rows: kv[rows, width:],
        refs, (ctx_t, None, None, None, lse),
    )


def middle_kernel(
    early, arrived, low, high, take, xh, kv, q_t, k_t, v_t, ctx_early, w_out,
    gh, d_t, dq_t, dk_t, dv_t, grad_out, back, back_low, back_high,
    spots, ctx_t, y, *work,
):
    cells, width = xh.shape
    spill = back_low.shape[0]
    done = early * (width // HEADS)
    pool_pick(take, arrived, low[:, width:], high[:, width:], spots, gh)
    d_t[...] = nt(w_out[...], gh[...]).astype(bf16)
    q_zero, d_zero, score, expd, dprob, prob, dscore, stat, acc_v, acc_k = work
    refs = (q_t, k_t, v_t, d_t, q_zero, d_zero, score, expd, dprob, prob, dscore, stat, acc_v, acc_k)
    attend(
        "both", early, HEADS - early,
        lambda rows: kv[rows, :width], lambda rows: kv[rows, width:],
        refs, (ctx_t, dq_t, dk_t, dv_t, None),
    )
    ctx_t[:done, :] = ctx_early[:done, :]
    grad_out[...] = nn(ctx_t[:width, :], gh[...])
    y[...] = (xh[...].astype(f32) + tn(ctx_t[:width, :], w_out[...])).astype(bf16)
    pool_place(take, y, back)
    tail = rows_at(take, y, back.shape[0], 2 * spill)
    back_low[...] = tail[:spill]
    back_high[...] = tail[spill:]


def backward_kernel(
    early, kv, q_t, k_t, v_t, d_t, lse, dq_late, dk_late, dv_late,
    d_qkv, dq_t, dk_t, dv_t, *work,
):
    width = q_t.shape[0]
    done = early * (width // HEADS)
    q_zero, d_zero, score, expd, dprob, prob, dscore, stat, acc_v, acc_k = work
    refs = (q_t, k_t, v_t, d_t, q_zero, d_zero, score, expd, dprob, prob, dscore, stat, acc_v, acc_k)
    attend(
        "backward", 0, early,
        lambda rows: kv[rows, :width], lambda rows: kv[rows, width:],
        refs, (None, dq_t, dk_t, dv_t, lse),
    )
    for i, (new, late) in enumerate(((dq_t, dq_late), (dk_t, dk_late), (dv_t, dv_late))):
        d_qkv[i * width : i * width + done, :] = new[:done, :]
        d_qkv[i * width + done : (i + 1) * width, :] = late[done:width, :]


def close_kernel(
    core, take, xh, gh, d_qkv, grad_out, y_low, y_high, gain, w_t,
    back, back_low, back_high, keep, give,
    dx, sums,
):
    cells, width = xh.shape
    spill = back_low.shape[0]
    xhat, rstd, normed = normalized(xh[...], gain[...])
    dn = tn(d_qkv[...], w_t[...])
    part_gain = jnp.sum(dn * xhat, axis=0, keepdims=True)
    sums[:, : 3 * width] = nn(d_qkv[...], normed).T
    sums[:, 3 * width : 4 * width] = grad_out[...]
    sums[:, 4 * width :] = jnp.broadcast_to(part_gain, (LANES, width)).T
    half = width // 2
    mine = core[0]
    keep[...] = sums[pl.ds(pl.multiple_of(mine * half, half), half), :]
    give[...] = sums[pl.ds(pl.multiple_of((1 - mine) * half, half), half), :]
    dxhat = dn * gain[...]
    inner = (
        dxhat
        - jnp.mean(dxhat, axis=-1, keepdims=True)
        - xhat * jnp.mean(dxhat * xhat, axis=-1, keepdims=True)
    )
    dx[...] = (gh[...].astype(f32) + inner * rstd).astype(bf16)
    pool_place(take, dx, back)
    tail = rows_at(take, dx, back.shape[0], 2 * spill)
    back_low[:, :width] = y_low[...]
    back_high[:, :width] = y_high[...]
    back_low[:, width:] = tail[:spill]
    back_high[:, width:] = tail[spill:]


def home_kernel(slot, y_arrived, dx_arrived, first, second, out, grad, spots):
    width = out.shape[1]
    spread_slots(slot, spots)
    edge = jnp.concatenate([first[...], second[...]], axis=0)
    for start in range(0, out.shape[0], LANES):
        rows = slice(start, start + LANES)
        main, rest = picks(spots, rows, y_arrived.shape[0], edge.shape[0])
        tail = nn(rest, edge)
        out[rows, :] = (nn(main, y_arrived[...]) + tail[:, :width]).astype(bf16)
        grad[rows, :] = (nn(main, dx_arrived[...]) + tail[:, width:]).astype(bf16)


def split_kernel(count, spot, *refs):
    parts, outs, total = refs[:count], refs[count:-1], refs[-1]
    total[...] = sum(part[...] for part in parts[1:]) + parts[0][...]
    ways = len(outs)
    share = total.shape[0] // ways
    for k, out in enumerate(outs):
        start = lax.rem(spot[0] + k, ways) * share
        out[...] = total[pl.ds(pl.multiple_of(start, share), share), :]


def repeat_kernel(*refs):
    out = refs[-1]
    total = sum(part[...] for part in refs[:-1])
    for k in range(out.shape[0]):
        out[k] = total


def add_kernel(scale, parts, out):
    total = parts[0]
    for k in range(1, parts.shape[0]):
        total = total + parts[k]
    out[...] = total * scale


def join_kernel(spot, *refs):
    parts, out = refs[:-1], refs[-1]
    ways = len(parts)
    share = parts[0].shape[0]
    for k, part in enumerate(parts):
        start = lax.rem(spot[0] + ways - k, ways) * share
        out[pl.ds(pl.multiple_of(start, share), share), :] = part[...]


def finish_kernel(core, mine, other, grad_qkv, grad_out, grad_gain, total):
    width = grad_out.shape[1]
    half = mine.shape[0]
    total[pl.ds(pl.multiple_of(core[0] * half, half), half), :] = mine[...]
    total[pl.ds(pl.multiple_of((1 - core[0]) * half, half), half), :] = other[...]
    grad_qkv[...] = total[:, : 3 * width]
    grad_out[...] = total[:, 3 * width : 4 * width]
    grad_gain[...] = total[:, 4 * width :].T[:1, :]


def permuted(value, axis, target):
    count = lax.axis_size(axis)
    return lax.ppermute(value, axis, [(s, target(s) % count) for s in range(count)])


def all_to_all(value, axis, groups=None):
    return lax.all_to_all(
        value, axis, split_axis=0, concat_axis=0, tiled=True, axis_index_groups=groups
    )


def call(body, outs, scratch, args, flops, name, smem=False, space=58):
    shapes = [jax.ShapeDtypeStruct(s, d) for s, d in outs]
    return pl.pallas_call(
        body,
        out_shape=shapes,
        in_specs=[
            pl.BlockSpec(memory_space=pltpu.SMEM if smem and i == 0 else pltpu.VMEM)
            for i in range(len(args))
        ],
        out_specs=[pl.BlockSpec(memory_space=pltpu.VMEM)] * len(shapes),
        scratch_shapes=[pltpu.VMEM(s, d) for s, d in scratch],
        compiler_params=pltpu.CompilerParams(vmem_limit_bytes=space * 2**20),
        cost_estimate=pl.CostEstimate(flops=flops, bytes_accessed=2**21, transcendentals=0),
        name=name,
    )(*args)


def after(value, *others):
    return lax.optimization_barrier((value, *others))[0]


def on_device(feats, dest, anchor, ln_gain, w_qkv, w_out, cotangent):
    cells, width = feats.shape
    groups = lax.axis_size("grp")
    segments = lax.axis_size("seg")
    spill = cells // 16
    room = 2 * (cells - 2 * spill) // groups
    flat = groups * room
    early = 12
    row_i = ((1, cells), jnp.int32)
    rows_b = ((cells, width), bf16)
    turned = ((width, cells), bf16)
    heads_t = ((width + width // HEADS, cells), bf16)
    leg = ((flat, width), bf16)
    edge = ((spill, width), bf16)
    edges = ((spill, 2 * width), bf16)
    spots = ((cells, LANES), jnp.int32)
    zeroed = ((2, width, cells), bf16)
    tile_f = ((2, cells, PART), f32)
    tile_b = ((2, cells, PART), bf16)
    stat = ((5, 2, 8, PART), f32)
    acc = ((width // HEADS, cells), f32)
    work = [zeroed, zeroed, tile_f, tile_f, tile_f, tile_b, tile_b, stat, acc, acc]
    seg = lax.axis_index("seg").astype(jnp.int32)
    core = (seg % 2).reshape(1)
    gain = ln_gain.reshape(1, width)
    w_t = w_qkv.T

    def exchange(rows):
        return all_to_all(rows.reshape(groups, room, width), "grp").reshape(flat, width)

    sizes = (segments, groups, room, spill)
    seg_ref = seg.reshape(1)
    home, x_out = call(
        lambda *refs: plan_kernel(*sizes, *refs), [row_i, leg], [],
        (seg_ref, dest.reshape(1, cells), feats), 2**32, "plan", smem=True,
    )
    x_in = exchange(x_out)
    take, g_out, up, down = call(
        lambda *refs: send_kernel(*sizes, *refs), [row_i, leg, edges, edges], [],
        (seg_ref, anchor.reshape(1, cells), home, feats, cotangent), 2**32, "send", smem=True,
    )
    low = permuted(up, "seg", lambda s: s + 1)
    high = permuted(down, "seg", lambda s: s - 1)
    g_in = exchange(after(g_out, x_in, low, high))
    xh, kv, q_t, k_t, v_t, ctx_t, lse = call(
        lambda *refs: forward_kernel(early, *refs),
        [rows_b, ((cells, 2 * width), bf16), turned, turned, turned, heads_t, ((HEADS * 8, cells), f32)],
        [spots, zeroed, tile_f, tile_f, tile_b, stat],
        (x_in, low, high, take, gain, w_qkv, w_t), 2**34, "forward",
    )
    gh, d_t, dq_t, dk_t, dv_t, grad_out, y_out, y_low, y_high = call(
        lambda *refs: middle_kernel(early, *refs),
        [rows_b, turned, heads_t, heads_t, heads_t, ((width, width), f32), leg, edge, edge],
        [spots, heads_t, rows_b, *work],
        (g_in, low, high, take, xh, kv, q_t, k_t, v_t, ctx_t, w_out), 2**35, "middle",
    )
    y_in = exchange(y_out)
    half = width // 2
    wide = 4 * width + LANES
    halves = ((half, wide), f32)
    (d_qkv,) = call(
        lambda *refs: backward_kernel(early, *refs),
        [((3 * width, cells), bf16)],
        [heads_t, heads_t, heads_t, *work],
        (kv, q_t, k_t, v_t, d_t, lse, dq_t, dk_t, dv_t), 2**35, "backward",
    )
    d_out, d_low, d_high, keep, give = call(
        close_kernel,
        [leg, edges, edges, halves, halves],
        [rows_b, ((width, wide), f32)],
        (core, take, xh, gh, after(d_qkv, y_in), grad_out, y_low, y_high, gain, w_t),
        2**32, "close", smem=True,
    )
    d_in = exchange(d_out)
    above = permuted(d_low, "seg", lambda s: s - 1)
    below = permuted(d_high, "seg", lambda s: s + 1)

    depth = 4
    rows_x, rows_y = half // depth, half // depth**2
    other = lambda s: s + 1 - 2 * (s % 2)
    ahead_x = lambda k: lambda s: (s // 2 + k) % depth * 2 + s % 2
    ahead_y = lambda k: lambda g: g // depth * depth + (g % depth + k) % depth
    lines = [list(range(y, groups, depth)) for y in range(depth)]
    spot_x = (seg // 2).reshape(1)
    spot_y = (lax.axis_index("grp").astype(jnp.int32) % depth).reshape(1)

    def split(parts, spot, share):
        count = len(parts)
        own, *rest = call(
            lambda *refs: split_kernel(count, *refs),
            [((share, wide), f32)] * depth, [((share * depth, wide), f32)],
            (spot, *parts), 2**28, "split", smem=True, space=16,
        )
        return own, rest

    def join(parts, spot, share):
        return call(
            join_kernel, [((share * depth, wide), f32)], [], (spot, *parts), 2**28, "join", smem=True, space=16
        )[0]

    own, rest = split([keep, permuted(give, "seg", other)], spot_x, rows_x)
    rest = [permuted(part, "seg", ahead_x(k + 1)) for k, part in enumerate(rest)]
    own, rest = split([own, *rest], spot_y, rows_y)
    rest = [permuted(part, "grp", ahead_y(k + 1)) for k, part in enumerate(rest)]
    stack = ((groups // depth, rows_y, wide), f32)
    pieces = call(repeat_kernel, [stack], [], (own, *rest), 2**28, "repeat", space=16)[0]
    pieces = after(pieces, d_in, above, below)
    landed = all_to_all(pieces, "grp", lines)
    factor = (cells * segments * groups) ** -0.5
    mine = call(
        lambda *refs: add_kernel(factor, *refs), [((rows_y, wide), f32)], [], (landed,), 2**28, "add", space=16
    )[0]
    mine = join([mine, *(permuted(mine, "grp", ahead_y(k)) for k in range(1, depth))], spot_y, rows_y)
    mine = join([mine, *(permuted(mine, "seg", ahead_x(k)) for k in range(1, depth))], spot_x, rows_x)
    theirs = permuted(mine, "seg", other)
    out_feats, grad_feats = call(
        home_kernel, [rows_b, rows_b], [spots], (home, y_in, d_in, above, below), 2**32, "home"
    )
    grad_qkv, grad_out, grad_gain = call(
        finish_kernel,
        [((width, 3 * width), f32), ((width, width), f32), ((1, width), f32)],
        [((width, wide), f32)], (core, mine, theirs), 2**24, "finish", smem=True, space=16,
    )
    return out_feats, grad_feats, grad_qkv, grad_out, grad_gain.reshape(width)


def solution(mesh):
    split = P(("seg", "grp"), None)
    line = P(("seg", "grp"))
    return jax.shard_map(
        on_device,
        mesh=mesh,
        in_specs=(split, line, line, P(), P(), P(), split),
        out_specs=(split, split, P(), P(), P()),
        check_vma=False,
    )
```

```python
import jax
import jax.numpy as jnp
from jax import lax
from jax.experimental import pallas as pl
from jax.experimental.pallas import tpu as pltpu
from jax.sharding import PartitionSpec as P

HEADS = 16
LANES = 128
PART = 256
f32 = jnp.float32
bf16 = jnp.bfloat16


def nn(a, b):
    return lax.dot_general(a, b, (((1,), (0,)), ((), ())), preferred_element_type=f32)


def nt(a, b):
    return lax.dot_general(a, b, (((1,), (1,)), ((), ())), preferred_element_type=f32)


def tn(a, b):
    return lax.dot_general(a, b, (((0,), (0,)), ((), ())), preferred_element_type=f32)


def column_of(row):
    return jnp.broadcast_to(row, (8, row.shape[1])).T[:, :1]


def one_hot(mark, like):
    return jnp.where(mark == like, 1.0, 0.0).astype(bf16)


def slots_of(value, seg, segments, groups, room, spill):
    cells = value.shape[1]
    owner = lax.div(value, cells)
    owner_seg = lax.div(owner, groups)
    owner_grp = owner - owner_seg * groups
    first = lax.rem(seg + 1, segments)
    inside = owner_seg == seg
    is_first = owner_seg == first
    bucket = jnp.where(inside, owner_grp, jnp.where(is_first, groups, groups + 1))
    flat = groups * room
    base = jnp.where(inside, owner_grp * room, jnp.where(is_first, flat, flat + spill))
    return bucket, base


def ranks_of(bucket, order):
    cells = bucket.shape[1]
    bucket_col = column_of(bucket.astype(f32))
    order_col = column_of(order.astype(f32))
    bucket_row = bucket.astype(f32)
    order_row = order.astype(f32)
    total = jnp.zeros((8, cells), f32)
    for start in range(0, cells, 8):
        same = bucket_col[start : start + 8] == bucket_row
        ahead = order_col[start : start + 8] < order_row
        total = total + jnp.where(same & ahead, 1.0, 0.0)
    return jnp.sum(total, axis=0, keepdims=True).astype(jnp.int32)


def picks(spots, rows, flat, tail):
    mine = spots[rows, :1]
    main = one_hot(lax.broadcasted_iota(jnp.int32, (LANES, flat), 1), mine)
    rest = one_hot(lax.broadcasted_iota(jnp.int32, (LANES, tail), 1) + flat, mine)
    return main, rest


def spread_slots(slot_row, spots):
    spots[...] = jnp.broadcast_to(
        column_of(slot_row[...].astype(f32)).astype(jnp.int32), spots.shape
    )


def pool_pick(slot_row, arrived, first, second, spots, target):
    spread_slots(slot_row, spots)
    edge = jnp.concatenate([first, second], axis=0)
    for start in range(0, target.shape[0], LANES):
        rows = slice(start, start + LANES)
        main, rest = picks(spots, rows, arrived.shape[0], edge.shape[0])
        target[rows, :] = (nn(main, arrived[...]) + nn(rest, edge)).astype(bf16)


def rows_at(slot_row, rows, start, count):
    spots = lax.broadcasted_iota(jnp.int32, (count, rows.shape[0]), 0) + start
    return nn(one_hot(spots, slot_row[...]), rows[...]).astype(bf16)


def pool_place(slot_row, rows, out):
    for start in range(0, out.shape[0], PART):
        out[start : start + PART, :] = rows_at(slot_row, rows, start, PART)


def plan_kernel(segments, groups, room, spill, seg_ref, dest, feats, home, out):
    index = lax.broadcasted_iota(jnp.int32, dest.shape, 1)
    bucket, base = slots_of(dest[...], seg_ref[0], segments, groups, room, spill)
    home[...] = base + ranks_of(bucket, index)
    pool_place(home, feats, out)


def send_kernel(segments, groups, room, spill, seg_ref, anchor, home, feats, cot, w_qkv, take, out, up, down, w_t):
    width = feats.shape[1]
    flat = groups * room
    w_t[...] = w_qkv[...].astype(f32).T.astype(bf16)
    for rows, lanes in ((feats, slice(0, width)), (cot, slice(width, 2 * width))):
        tail = rows_at(home, rows, flat, 2 * spill)
        up[:, lanes] = tail[:spill]
        down[:, lanes] = tail[spill:]
    source = anchor[...]
    bucket, base = slots_of(source, seg_ref[0], segments, groups, room, spill)
    base = jnp.where(
        bucket == groups + 1, flat, jnp.where(bucket == groups, flat + spill, base)
    )
    take[...] = base + ranks_of(bucket, source)
    pool_place(home, cot, out)


def normalized(x, gain):
    xf = x.astype(f32)
    centered = xf - jnp.mean(xf, axis=-1, keepdims=True)
    rstd = lax.rsqrt(jnp.mean(centered * centered, axis=-1, keepdims=True) + 1e-05)
    xhat = centered * rstd
    return xhat, rstd, (xhat * gain).astype(bf16)


def attend(mode, first, count, k_all, v_all, refs, outs):
    q_t, k_t, v_t, d_t, q_zero, d_zero, score, expd, dprob, prob, dscore, stat, acc_v, acc_k = refs
    ctx_t, dq_t, dk_t, dv_t, lse = outs
    cells = score.shape[1]
    blocks = cells // PART
    size = q_t.shape[0] // HEADS
    backward = mode != "forward"
    forward = mode != "backward"
    last = first + count - 1
    TOP, SUM, INV, DOT, INNER = range(5)

    def rows(head):
        return pl.ds(pl.multiple_of(head * size, size), size)

    def rows8(head):
        return pl.ds(pl.multiple_of(head * 8, 8), 8)

    def part(index):
        return slice(index * PART, (index + 1) * PART)

    def fold(op, tile):
        return op(tile.reshape(PART // 8, 8, PART), axis=0)

    def combine(kind, block, piece, value, op):
        if piece:
            value = op(stat[kind, block % 2], value)
        stat[kind, block % 2] = value

    def spread(row):
        return jnp.broadcast_to(row, (8, PART))

    def set_head(head):
        slot = lax.rem(head, 2)
        old = rows(lax.rem(head + HEADS - 2, HEADS))
        new = rows(head)
        q_zero[slot, old, :] = jnp.zeros((size, cells), bf16)
        q_zero[slot, new, :] = q_t[new, :]
        if backward:
            d_zero[slot, old, :] = jnp.zeros((size, cells), bf16)
            d_zero[slot, new, :] = d_t[new, :]

    def stage_scores(head, block, piece):
        s = nn(k_all(part(piece)), q_zero[lax.rem(head, 2), :, part(block)])
        score[block % 2, part(piece), :] = s
        if forward:
            combine(TOP, block, piece, fold(jnp.max, s), jnp.maximum)
            if piece == blocks - 1:
                stat[TOP, block % 2] = spread(
                    jnp.max(stat[TOP, block % 2], axis=0, keepdims=True)
                )

    def stage_exp(head, block, piece):
        slot = block % 2
        top = stat[TOP, slot][:1] if forward else lse[rows8(head), part(block)][:1]
        e = jnp.exp(score[slot, part(piece), :] - top)
        expd[slot, part(piece), :] = e
        if forward:
            combine(SUM, block, piece, fold(jnp.sum, e), jnp.add)
        if backward:
            dp = nn(v_all(part(piece)), d_zero[lax.rem(head, 2), :, part(block)])
            dprob[slot, part(piece), :] = dp
            combine(DOT, block, piece, fold(jnp.sum, e * dp), jnp.add)
        if piece == blocks - 1:
            if forward:
                total = jnp.sum(stat[SUM, slot], axis=0, keepdims=True)
                inverse = 1.0 / total
                stat[INV, slot] = spread(inverse)
                if mode == "forward":
                    lse[rows8(head), part(block)] = spread(top + jnp.log(total))
            if backward:
                inner = jnp.sum(stat[DOT, slot], axis=0, keepdims=True)
                stat[INNER, slot] = spread(inner * inverse if forward else inner)

    def stage_probs(block, piece):
        slot = block % 2
        p = expd[slot, part(piece), :]
        if forward:
            p = p * stat[INV, slot][:1]
        prob[slot, part(piece), :] = p.astype(bf16)
        if backward:
            dp = dprob[slot, part(piece), :]
            dscore[slot, part(piece), :] = (p * (dp - stat[INNER, slot][:1])).astype(bf16)

    def stage_products(head, spot, block, piece):
        mine, out, slot, cols = rows(head), rows(spot), block % 2, part(block)
        if forward and piece == 0:
            ctx_t[out, cols] = nn(v_t[mine, :], prob[slot]).astype(bf16)
        if backward:
            if piece == 1:
                dq_t[out, cols] = nn(k_t[mine, :], dscore[slot]).astype(bf16)
            if piece == 2:
                more = nt(d_t[mine, cols], prob[slot])
                acc_v[...] = more if block == 0 else acc_v[...] + more
            if piece == 3:
                more = nt(q_t[mine, cols], dscore[slot])
                acc_k[...] = more if block == 0 else acc_k[...] + more
                if block == blocks - 1:
                    dv_t[out, :] = acc_v[...].astype(bf16)
                    dk_t[out, :] = acc_k[...].astype(bf16)

    def body(head, drain=False):
        before = lax.rem(head + HEADS - 1, HEADS)
        spot = jnp.where(head == first, HEADS, head - 1)
        for step in range(blocks - 1 if drain else blocks):
            for piece in range(blocks):
                late = step - 3
                if late < 0:
                    stage_products(before, spot, late + blocks, piece)
                elif not drain:
                    stage_products(head, head, late, piece)
                if not drain:
                    stage_scores(head, step, piece)
                late = step - 2
                if late < 0:
                    stage_probs(late + blocks, piece)
                elif not drain:
                    stage_probs(late, piece)
                late = step - 1
                if late < 0:
                    stage_exp(before, late + blocks, piece)
                elif not drain:
                    stage_exp(head, late, piece)

    def one_head(head, _):
        set_head(head)
        body(head)
        return 0

    q_zero[...] = jnp.zeros_like(q_zero)
    if backward:
        d_zero[...] = jnp.zeros_like(d_zero)
    lax.fori_loop(first, last + 1, one_head, 0)
    body(jnp.int32(last + 1), drain=True)


def forward_kernel(
    early, arrived, low, high, take, gain, w_qkv, w_t,
    xh, kv, q_t, k_t, v_t, ctx_t, lse,
    spots, *work,
):
    width = xh.shape[1]
    scale = (width // HEADS) ** -0.5
    pool_pick(take, arrived, low[:, :width], high[:, :width], spots, xh)
    _, _, normed = normalized(xh[...], gain[...])
    kv[...] = nn(normed, w_qkv[:, width:]).astype(bf16)
    q_t[...] = (nt(w_t[:width, :], normed).astype(bf16).astype(f32) * scale).astype(bf16)
    k_t[...] = (nt(w_t[width : 2 * width, :], normed).astype(bf16).astype(f32) * scale).astype(bf16)
    v_t[...] = nt(w_t[2 * width :, :], normed).astype(bf16)
    q_zero, score, expd, prob, stat = work
    refs = (q_t, k_t, v_t, None, q_zero, None, score, expd, None, prob, None, stat, None, None)
    attend(
        "forward", 0, early,
        lambda rows: kv[rows, :width], lambda rows: kv[rows, width:],
        refs, (ctx_t, None, None, None, lse),
    )


def backward_kernel(
    early, core, arrived, low, high, take, xh, kv, q_t, k_t, v_t, ctx_early, lse, gain, w_t, w_out,
    back, back_low, back_high, keep, give,
    spots, gh, d_t, d_qkv, ctx_t, dq_t, dk_t, dv_t, done, sums, *work,
):
    cells, width = xh.shape
    size = width // HEADS
    spill = back_low.shape[0]
    pool_pick(take, arrived, low[:, width:], high[:, width:], spots, gh)
    d_t[...] = nt(w_out[...], gh[...]).astype(bf16)
    q_zero, d_zero, score, expd, dprob, prob, dscore, stat, acc_v, acc_k = work
    refs = (q_t, k_t, v_t, d_t, q_zero, d_zero, score, expd, dprob, prob, dscore, stat, acc_v, acc_k)
    keys, values = lambda rows: kv[rows, :width], lambda rows: kv[rows, width:]
    attend("both", early, HEADS - early, keys, values, refs, (ctx_t, dq_t, dk_t, dv_t, None))
    attend("backward", 0, early, keys, values, refs, (None, dq_t, dk_t, dv_t, lse))
    ctx_t[: early * size, :] = ctx_early[: early * size, :]
    for i, part in enumerate((dq_t, dk_t, dv_t)):
        d_qkv[i * width : (i + 1) * width, :] = part[:width, :]
    xhat, rstd, normed = normalized(xh[...], gain[...])
    dn = tn(d_qkv[...], w_t[...])
    part_gain = jnp.sum(dn * xhat, axis=0, keepdims=True)
    sums[:, : 3 * width] = nn(d_qkv[...], normed).T
    sums[:, 3 * width : 4 * width] = nn(ctx_t[:width, :], gh[...])
    sums[:, 4 * width :] = jnp.broadcast_to(part_gain, (LANES, width)).T
    half = width // 2
    mine = core[0]
    keep[...] = sums[pl.ds(pl.multiple_of(mine * half, half), half), :]
    give[...] = sums[pl.ds(pl.multiple_of((1 - mine) * half, half), half), :]
    dxhat = dn * gain[...]
    inner = (
        dxhat
        - jnp.mean(dxhat, axis=-1, keepdims=True)
        - xhat * jnp.mean(dxhat * xhat, axis=-1, keepdims=True)
    )
    done[:, :width] = (xh[...].astype(f32) + tn(ctx_t[:width, :], w_out[...])).astype(bf16)
    done[:, width:] = (gh[...].astype(f32) + inner * rstd).astype(bf16)
    pool_place(take, done, back)
    tail = rows_at(take, done, back.shape[0], 2 * spill)
    back_low[...] = tail[:spill]
    back_high[...] = tail[spill:]


def home_kernel(slot, arrived, first, second, out, grad, spots):
    width = out.shape[1]
    spread_slots(slot, spots)
    edge = jnp.concatenate([first[...], second[...]], axis=0)
    for start in range(0, out.shape[0], LANES):
        rows = slice(start, start + LANES)
        main, rest = picks(spots, rows, arrived.shape[0], edge.shape[0])
        both = nn(main, arrived[...]) + nn(rest, edge)
        out[rows, :] = both[:, :width].astype(bf16)
        grad[rows, :] = both[:, width:].astype(bf16)


def split_kernel(count, spot, *refs):
    parts, outs, total = refs[:count], refs[count:-1], refs[-1]
    total[...] = sum(part[...] for part in parts[1:]) + parts[0][...]
    ways = len(outs)
    share = total.shape[0] // ways
    for k, out in enumerate(outs):
        start = lax.rem(spot[0] + k, ways) * share
        out[...] = total[pl.ds(pl.multiple_of(start, share), share), :]


def join_kernel(spot, *refs):
    parts, out = refs[:-1], refs[-1]
    ways = len(parts)
    share = parts[0].shape[0]
    for k, part in enumerate(parts):
        start = lax.rem(spot[0] + ways - k, ways) * share
        out[pl.ds(pl.multiple_of(start, share), share), :] = part[...]


def finish_kernel(factor, core, mine, other, grad_qkv, grad_out, grad_gain, total):
    width = grad_out.shape[1]
    half = mine.shape[0]
    total[pl.ds(pl.multiple_of(core[0] * half, half), half), :] = mine[...] * factor
    total[pl.ds(pl.multiple_of((1 - core[0]) * half, half), half), :] = other[...] * factor
    grad_qkv[...] = total[:, : 3 * width]
    grad_out[...] = total[:, 3 * width : 4 * width]
    grad_gain[...] = total[:, 4 * width :].T[:1, :]


def permuted(value, axis, target):
    count = lax.axis_size(axis)
    return lax.ppermute(value, axis, [(s, target(s) % count) for s in range(count)])


def all_to_all(value, axis, groups=None):
    return lax.all_to_all(
        value, axis, split_axis=0, concat_axis=0, tiled=True, axis_index_groups=groups
    )


def call(body, outs, scratch, args, flops, name, smem=False, space=58):
    shapes = [jax.ShapeDtypeStruct(s, d) for s, d in outs]
    return pl.pallas_call(
        body,
        out_shape=shapes,
        in_specs=[
            pl.BlockSpec(memory_space=pltpu.SMEM if smem and i == 0 else pltpu.VMEM)
            for i in range(len(args))
        ],
        out_specs=[pl.BlockSpec(memory_space=pltpu.VMEM)] * len(shapes),
        scratch_shapes=[pltpu.VMEM(s, d) for s, d in scratch],
        compiler_params=pltpu.CompilerParams(vmem_limit_bytes=space * 2**20),
        cost_estimate=pl.CostEstimate(flops=flops, bytes_accessed=2**21, transcendentals=0),
        name=name,
    )(*args)


def after(value, *others):
    return lax.optimization_barrier((value, *others))[0]


def on_device(feats, dest, anchor, ln_gain, w_qkv, w_out, cotangent):
    cells, width = feats.shape
    groups = lax.axis_size("grp")
    segments = lax.axis_size("seg")
    spill = cells // 16
    room = 2 * (cells - 2 * spill) // groups
    flat = groups * room
    early = 12
    row_i = ((1, cells), jnp.int32)
    rows_b = ((cells, width), bf16)
    turned = ((width, cells), bf16)
    heads_t = ((width + width // HEADS, cells), bf16)
    leg = ((flat, width), bf16)
    edge = ((spill, width), bf16)
    edges = ((spill, 2 * width), bf16)
    spots = ((cells, LANES), jnp.int32)
    zeroed = ((2, width, cells), bf16)
    tile_f = ((2, cells, PART), f32)
    tile_b = ((2, cells, PART), bf16)
    stat = ((5, 2, 8, PART), f32)
    acc = ((width // HEADS, cells), f32)
    work = [zeroed, zeroed, tile_f, tile_f, tile_f, tile_b, tile_b, stat, acc, acc]
    seg = lax.axis_index("seg").astype(jnp.int32)
    core = (seg % 2).reshape(1)
    gain = ln_gain.reshape(1, width)

    def exchange(rows):
        return all_to_all(rows.reshape(groups, room, -1), "grp").reshape(rows.shape)

    sizes = (segments, groups, room, spill)
    seg_ref = seg.reshape(1)
    home, x_out = call(
        lambda *refs: plan_kernel(*sizes, *refs), [row_i, leg], [],
        (seg_ref, dest.reshape(1, cells), feats), 2**32, "plan", smem=True,
    )
    x_in = exchange(x_out)
    take, g_out, up, down, w_t = call(
        lambda *refs: send_kernel(*sizes, *refs), [row_i, leg, edges, edges, ((3 * width, width), bf16)], [],
        (seg_ref, anchor.reshape(1, cells), home, feats, cotangent, w_qkv), 2**32, "send", smem=True,
    )
    low = permuted(up, "seg", lambda s: s + 1)
    high = permuted(down, "seg", lambda s: s - 1)
    g_in = exchange(after(g_out, x_in, low, high))
    xh, kv, q_t, k_t, v_t, ctx_t, lse = call(
        lambda *refs: forward_kernel(early, *refs),
        [rows_b, ((cells, 2 * width), bf16), turned, turned, turned, heads_t, ((HEADS * 8, cells), f32)],
        [spots, zeroed, tile_f, tile_f, tile_b, stat],
        (x_in, low, high, take, gain, w_qkv, w_t), 2**34, "forward",
    )
    half = width // 2
    wide = 4 * width + LANES
    halves = ((half, wide), f32)
    done, d_low, d_high, keep, give = call(
        lambda *refs: backward_kernel(early, *refs),
        [((flat, 2 * width), bf16), edges, edges, halves, halves],
        [
            spots, rows_b, turned, ((3 * width, cells), bf16), heads_t, heads_t, heads_t, heads_t,
            ((cells, 2 * width), bf16), ((width, wide), f32), *work,
        ],
        (core, g_in, low, high, take, xh, kv, q_t, k_t, v_t, ctx_t, lse, gain, w_t, w_out),
        2**36, "backward", smem=True,
    )
    done_in = exchange(done)
    above = permuted(d_low, "seg", lambda s: s - 1)
    below = permuted(d_high, "seg", lambda s: s + 1)

    depth = 4
    rows_x, rows_y = half // depth, half // depth**2
    other = lambda s: s + 1 - 2 * (s % 2)
    ahead_x = lambda k: lambda s: (s // 2 + k) % depth * 2 + s % 2
    ahead_y = lambda k: lambda g: g // depth * depth + (g % depth + k) % depth
    spot_x = (seg // 2).reshape(1)
    spot_y = (lax.axis_index("grp").astype(jnp.int32) % depth).reshape(1)

    def split(parts, spot, share):
        count = len(parts)
        own, *rest = call(
            lambda *refs: split_kernel(count, *refs),
            [((share, wide), f32)] * depth, [((share * depth, wide), f32)],
            (spot, *parts), 2**28, "split", smem=True, space=16,
        )
        return own, rest

    def join(parts, spot, share):
        return call(
            join_kernel, [((share * depth, wide), f32)], [], (spot, *parts), 2**28, "join", smem=True, space=16
        )[0]

    own, rest = split([keep, permuted(give, "seg", other)], spot_x, rows_x)
    rest = [permuted(part, "seg", ahead_x(k + 1)) for k, part in enumerate(rest)]
    own, rest = split([own, *rest], spot_y, rows_y)
    rest = [permuted(part, "grp", ahead_y(k + 1)) for k, part in enumerate(rest)]
    mine = call(
        lambda *refs: split_kernel(depth, *refs), [((rows_y, wide), f32)], [((rows_y, wide), f32)],
        (spot_y, own, *rest), 2**28, "sum", smem=True, space=16,
    )[0]
    step = 1
    while step < groups // depth:
        mine = mine + permuted(mine, "grp", lambda g, step=step: g ^ (step * depth))
        step *= 2
    mine = after(mine, done_in, above, below)
    mine = join([mine, *(permuted(mine, "grp", ahead_y(k)) for k in range(1, depth))], spot_y, rows_y)
    mine = join([mine, *(permuted(mine, "seg", ahead_x(k)) for k in range(1, depth))], spot_x, rows_x)
    theirs = permuted(mine, "seg", other)
    out_feats, grad_feats = call(
        home_kernel, [rows_b, rows_b], [spots], (home, done_in, above, below), 2**32, "home"
    )
    grad_qkv, grad_out, grad_gain = call(
        lambda *refs: finish_kernel((cells * segments * groups) ** -0.5, *refs),
        [((width, 3 * width), f32), ((width, width), f32), ((1, width), f32)],
        [((width, wide), f32)], (core, mine, theirs), 2**24, "finish", smem=True, space=16,
    )
    return out_feats, grad_feats, grad_qkv, grad_out, grad_gain.reshape(width)


def solution(mesh):
    split = P(("seg", "grp"), None)
    line = P(("seg", "grp"))
    return jax.shard_map(
        on_device,
        mesh=mesh,
        in_specs=(split, line, line, P(), P(), P(), split),
        out_specs=(split, split, P(), P(), P()),
        check_vma=False,
    )
```

```python
import jax
import jax.numpy as jnp
from jax import lax
from jax.experimental import pallas as pl
from jax.experimental.pallas import tpu as pltpu
from jax.sharding import PartitionSpec as P

HEADS = 16
LANES = 128
PART = 256
f32 = jnp.float32
bf16 = jnp.bfloat16


def nn(a, b):
    return lax.dot_general(a, b, (((1,), (0,)), ((), ())), preferred_element_type=f32)


def nt(a, b):
    return lax.dot_general(a, b, (((1,), (1,)), ((), ())), preferred_element_type=f32)


def tn(a, b):
    return lax.dot_general(a, b, (((0,), (0,)), ((), ())), preferred_element_type=f32)


def column_of(row):
    return jnp.broadcast_to(row, (8, row.shape[1])).T[:, :1]


def one_hot(mark, like):
    return jnp.where(mark == like, 1.0, 0.0).astype(bf16)


def slots_of(value, seg, segments, groups, room, spill):
    cells = value.shape[1]
    owner = lax.div(value, cells)
    owner_seg = lax.div(owner, groups)
    owner_grp = owner - owner_seg * groups
    first = lax.rem(seg + 1, segments)
    inside = owner_seg == seg
    is_first = owner_seg == first
    bucket = jnp.where(inside, owner_grp, jnp.where(is_first, groups, groups + 1))
    flat = groups * room
    base = jnp.where(inside, owner_grp * room, jnp.where(is_first, flat, flat + spill))
    return bucket, base


def ranks_of(bucket, order):
    cells = bucket.shape[1]
    bucket_col = column_of(bucket.astype(f32))
    order_col = column_of(order.astype(f32))
    bucket_row = bucket.astype(f32)
    order_row = order.astype(f32)
    total = jnp.zeros((8, cells), f32)
    for start in range(0, cells, 8):
        same = bucket_col[start : start + 8] == bucket_row
        ahead = order_col[start : start + 8] < order_row
        total = total + jnp.where(same & ahead, 1.0, 0.0)
    return jnp.sum(total, axis=0, keepdims=True).astype(jnp.int32)


def picks(spots, rows, flat, tail):
    mine = spots[rows, :1]
    main = one_hot(lax.broadcasted_iota(jnp.int32, (LANES, flat), 1), mine)
    rest = one_hot(lax.broadcasted_iota(jnp.int32, (LANES, tail), 1) + flat, mine)
    return main, rest


def spread_slots(slot_row, spots):
    spots[...] = jnp.broadcast_to(
        column_of(slot_row[...].astype(f32)).astype(jnp.int32), spots.shape
    )


def pool_pick(slot_row, arrived, first, second, spots, target):
    spread_slots(slot_row, spots)
    edge = jnp.concatenate([first, second], axis=0)
    for start in range(0, target.shape[0], LANES):
        rows = slice(start, start + LANES)
        main, rest = picks(spots, rows, arrived.shape[0], edge.shape[0])
        target[rows, :] = (nn(main, arrived[...]) + nn(rest, edge)).astype(bf16)


def rows_at(slot_row, rows, start, count):
    spots = lax.broadcasted_iota(jnp.int32, (count, rows.shape[0]), 0) + start
    return nn(one_hot(spots, slot_row[...]), rows[...]).astype(bf16)


def pool_place(slot_row, rows, out):
    for start in range(0, out.shape[0], PART):
        out[start : start + PART, :] = rows_at(slot_row, rows, start, PART)


def plan_kernel(segments, groups, room, spill, seg_ref, dest, feats, home, out):
    index = lax.broadcasted_iota(jnp.int32, dest.shape, 1)
    bucket, base = slots_of(dest[...], seg_ref[0], segments, groups, room, spill)
    home[...] = base + ranks_of(bucket, index)
    pool_place(home, feats, out)


def send_kernel(segments, groups, room, spill, seg_ref, anchor, home, feats, cot, w_qkv, take, out, up, down, w_t):
    width = feats.shape[1]
    flat = groups * room
    w_t[...] = w_qkv[...].astype(f32).T.astype(bf16)
    for rows, lanes in ((feats, slice(0, width)), (cot, slice(width, 2 * width))):
        tail = rows_at(home, rows, flat, 2 * spill)
        up[:, lanes] = tail[:spill]
        down[:, lanes] = tail[spill:]
    source = anchor[...]
    bucket, base = slots_of(source, seg_ref[0], segments, groups, room, spill)
    base = jnp.where(
        bucket == groups + 1, flat, jnp.where(bucket == groups, flat + spill, base)
    )
    take[...] = base + ranks_of(bucket, source)
    pool_place(home, cot, out)


def normalized(x, gain):
    xf = x.astype(f32)
    centered = xf - jnp.mean(xf, axis=-1, keepdims=True)
    rstd = lax.rsqrt(jnp.mean(centered * centered, axis=-1, keepdims=True) + 1e-05)
    xhat = centered * rstd
    return xhat, rstd, (xhat * gain).astype(bf16)


def attend(runs, k_all, v_all, refs, outs):
    q_t, k_t, v_t, d_t, q_zero, d_zero, score, expd, dprob, prob, dscore, stat, acc_v, acc_k = refs
    ctx_t, dq_t, dk_t, dv_t, lse = outs
    cells = score.shape[1]
    blocks = cells // PART
    size = q_t.shape[0] // HEADS
    TOP, SUM, INV, DOT, INNER = range(5)

    def rows(head):
        return pl.ds(pl.multiple_of(head * size, size), size)

    def rows8(head):
        return pl.ds(pl.multiple_of(head * 8, 8), 8)

    def part(index):
        return slice(index * PART, (index + 1) * PART)

    def fold(op, tile):
        return op(tile.reshape(PART // 8, 8, PART), axis=0)

    def combine(kind, block, piece, value, op):
        if piece:
            value = op(stat[kind, block % 2], value)
        stat[kind, block % 2] = value

    def spread(row):
        return jnp.broadcast_to(row, (8, PART))

    def set_head(mode, head):
        slot = lax.rem(head, 2)
        old = rows(lax.rem(head + HEADS - 2, HEADS))
        new = rows(head)
        q_zero[slot, old, :] = jnp.zeros((size, cells), bf16)
        q_zero[slot, new, :] = q_t[new, :]
        if mode != "forward":
            d_zero[slot, old, :] = jnp.zeros((size, cells), bf16)
            d_zero[slot, new, :] = d_t[new, :]

    def stage_scores(mode, head, block, piece):
        forward = mode != "backward"
        s = nn(k_all(part(piece)), q_zero[lax.rem(head, 2), :, part(block)])
        score[block % 2, part(piece), :] = s
        if forward:
            combine(TOP, block, piece, fold(jnp.max, s), jnp.maximum)
            if piece == blocks - 1:
                stat[TOP, block % 2] = spread(
                    jnp.max(stat[TOP, block % 2], axis=0, keepdims=True)
                )

    def stage_exp(mode, head, block, piece):
        forward, backward = mode != "backward", mode != "forward"
        slot = block % 2
        top = stat[TOP, slot][:1] if forward else lse[rows8(head), part(block)][:1]
        e = jnp.exp(score[slot, part(piece), :] - top)
        expd[slot, part(piece), :] = e
        if forward:
            combine(SUM, block, piece, fold(jnp.sum, e), jnp.add)
        if backward:
            dp = nn(v_all(part(piece)), d_zero[lax.rem(head, 2), :, part(block)])
            dprob[slot, part(piece), :] = dp
            combine(DOT, block, piece, fold(jnp.sum, e * dp), jnp.add)
        if piece == blocks - 1:
            if forward:
                total = jnp.sum(stat[SUM, slot], axis=0, keepdims=True)
                inverse = 1.0 / total
                stat[INV, slot] = spread(inverse)
                if mode == "forward":
                    lse[rows8(head), part(block)] = spread(top + jnp.log(total))
            if backward:
                inner = jnp.sum(stat[DOT, slot], axis=0, keepdims=True)
                stat[INNER, slot] = spread(inner * inverse if forward else inner)

    def stage_probs(mode, block, piece):
        forward, backward = mode != "backward", mode != "forward"
        slot = block % 2
        p = expd[slot, part(piece), :]
        if forward:
            p = p * stat[INV, slot][:1]
        prob[slot, part(piece), :] = p.astype(bf16)
        if backward:
            dp = dprob[slot, part(piece), :]
            dscore[slot, part(piece), :] = (p * (dp - stat[INNER, slot][:1])).astype(bf16)

    def stage_products(mode, head, spot, block, piece):
        forward, backward = mode != "backward", mode != "forward"
        mine, out, slot, cols = rows(head), rows(spot), block % 2, part(block)
        if forward and piece == 0:
            ctx_t[out, cols] = nn(v_t[mine, :], prob[slot]).astype(bf16)
        if backward:
            if piece == 1:
                dq_t[out, cols] = nn(k_t[mine, :], dscore[slot]).astype(bf16)
            if piece == 2:
                more = nt(d_t[mine, cols], prob[slot])
                acc_v[...] = more if block == 0 else acc_v[...] + more
            if piece == 3:
                more = nt(q_t[mine, cols], dscore[slot])
                acc_k[...] = more if block == 0 else acc_k[...] + more
                if block == blocks - 1:
                    dv_t[out, :] = acc_v[...].astype(bf16)
                    dk_t[out, :] = acc_k[...].astype(bf16)

    def body(mode, head, was, before, spot):
        for step in range(blocks if mode else blocks - 1):
            for piece in range(blocks):
                late = step - 3
                if late < 0:
                    stage_products(was, before, spot, late + blocks, piece)
                elif mode:
                    stage_products(mode, head, head, late, piece)
                if mode:
                    stage_scores(mode, head, step, piece)
                late = step - 2
                if late < 0:
                    stage_probs(was, late + blocks, piece)
                elif mode:
                    stage_probs(mode, late, piece)
                late = step - 1
                if late < 0:
                    stage_exp(was, before, late + blocks, piece)
                elif mode:
                    stage_exp(mode, head, late, piece)

    q_zero[...] = jnp.zeros_like(q_zero)
    if d_zero is not None:
        d_zero[...] = jnp.zeros_like(d_zero)
    was = before = None
    for mode, first, count in runs:
        start = first if was is None else first + 1
        if was is not None:
            set_head(mode, jnp.int32(first))
            body(mode, jnp.int32(first), was, jnp.int32(before), jnp.int32(before))

        def one_head(head, _, mode=mode, alone=None if was else first):
            set_head(mode, head)
            spot = head - 1 if alone is None else jnp.where(head == alone, HEADS, head - 1)
            body(mode, head, mode, lax.rem(head + HEADS - 1, HEADS), spot)
            return 0

        lax.fori_loop(start, first + count, one_head, 0)
        was, before = mode, first + count - 1
    body(None, None, was, jnp.int32(before), jnp.int32(before))


def forward_kernel(
    early, arrived, low, high, take, gain, w_qkv, w_t,
    xh, kv, q_t, k_t, v_t, ctx_t, lse,
    spots, *work,
):
    width = xh.shape[1]
    scale = (width // HEADS) ** -0.5
    pool_pick(take, arrived, low[:, :width], high[:, :width], spots, xh)
    _, _, normed = normalized(xh[...], gain[...])
    kv[...] = nn(normed, w_qkv[:, width:]).astype(bf16)
    q_t[...] = (nt(w_t[:width, :], normed).astype(bf16).astype(f32) * scale).astype(bf16)
    k_t[...] = (nt(w_t[width : 2 * width, :], normed).astype(bf16).astype(f32) * scale).astype(bf16)
    v_t[...] = nt(w_t[2 * width :, :], normed).astype(bf16)
    q_zero, score, expd, prob, stat = work
    refs = (q_t, k_t, v_t, None, q_zero, None, score, expd, None, prob, None, stat, None, None)
    attend(
        [("forward", 0, early)],
        lambda rows: kv[rows, :width], lambda rows: kv[rows, width:],
        refs, (ctx_t, None, None, None, lse),
    )


def backward_kernel(
    early, core, arrived, low, high, take, xh, kv, q_t, k_t, v_t, ctx_early, lse, gain, w_t, w_out,
    back, back_low, back_high, keep, give,
    spots, gh, d_t, d_qkv, ctx_t, dq_t, dk_t, dv_t, done, sums, *work,
):
    cells, width = xh.shape
    size = width // HEADS
    spill = back_low.shape[0]
    pool_pick(take, arrived, low[:, width:], high[:, width:], spots, gh)
    d_t[...] = nt(w_out[...], gh[...]).astype(bf16)
    q_zero, d_zero, score, expd, dprob, prob, dscore, stat, acc_v, acc_k = work
    refs = (q_t, k_t, v_t, d_t, q_zero, d_zero, score, expd, dprob, prob, dscore, stat, acc_v, acc_k)
    keys, values = lambda rows: kv[rows, :width], lambda rows: kv[rows, width:]
    attend(
        [("both", early, HEADS - early), ("backward", 0, early)],
        keys, values, refs, (ctx_t, dq_t, dk_t, dv_t, lse),
    )
    ctx_t[: early * size, :] = ctx_early[: early * size, :]
    for i, part in enumerate((dq_t, dk_t, dv_t)):
        d_qkv[i * width : (i + 1) * width, :] = part[:width, :]
    xhat, rstd, normed = normalized(xh[...], gain[...])
    dn = tn(d_qkv[...], w_t[...])
    part_gain = jnp.sum(dn * xhat, axis=0, keepdims=True)
    sums[:, : 3 * width] = nn(d_qkv[...], normed).T
    sums[:, 3 * width : 4 * width] = nn(ctx_t[:width, :], gh[...])
    sums[:, 4 * width :] = jnp.broadcast_to(part_gain, (LANES, width)).T
    half = width // 2
    mine = core[0]
    keep[...] = sums[pl.ds(pl.multiple_of(mine * half, half), half), :]
    give[...] = sums[pl.ds(pl.multiple_of((1 - mine) * half, half), half), :]
    dxhat = dn * gain[...]
    inner = (
        dxhat
        - jnp.mean(dxhat, axis=-1, keepdims=True)
        - xhat * jnp.mean(dxhat * xhat, axis=-1, keepdims=True)
    )
    done[:, :width] = (xh[...].astype(f32) + tn(ctx_t[:width, :], w_out[...])).astype(bf16)
    done[:, width:] = (gh[...].astype(f32) + inner * rstd).astype(bf16)
    pool_place(take, done, back)
    tail = rows_at(take, done, back.shape[0], 2 * spill)
    back_low[...] = tail[:spill]
    back_high[...] = tail[spill:]


def home_kernel(side, slot, arrived, first, second, out, spots):
    width = out.shape[1]
    lanes = slice(side * width, (side + 1) * width)
    pool_pick(slot, arrived.at[:, lanes], first[:, lanes], second[:, lanes], spots, out)


def split_kernel(count, spot, *refs):
    parts, outs, total = refs[:count], refs[count:-1], refs[-1]
    total[...] = sum(part[...] for part in parts[1:]) + parts[0][...]
    ways = len(outs)
    share = total.shape[0] // ways
    for k, out in enumerate(outs):
        start = lax.rem(spot[0] + k, ways) * share
        out[...] = total[pl.ds(pl.multiple_of(start, share), share), :]


def order_kernel(spot, *refs):
    parts, out, stack = refs[:-2], refs[-2], refs[-1]
    ways = len(parts)
    for k, part in enumerate(parts):
        stack[lax.rem(spot[0] + ways - k, ways)] = part[...]
    total = stack[0]
    for k in range(1, ways):
        total = total + stack[k]
    out[...] = total


def join_kernel(spot, *refs):
    parts, out = refs[:-1], refs[-1]
    ways = len(parts)
    share = parts[0].shape[0]
    for k, part in enumerate(parts):
        start = lax.rem(spot[0] + ways - k, ways) * share
        out[pl.ds(pl.multiple_of(start, share), share), :] = part[...]


def finish_kernel(factor, core, mine, other, grad_qkv, grad_out, grad_gain, total):
    width = grad_out.shape[1]
    half = mine.shape[0]
    total[pl.ds(pl.multiple_of(core[0] * half, half), half), :] = mine[...] * factor
    total[pl.ds(pl.multiple_of((1 - core[0]) * half, half), half), :] = other[...] * factor
    grad_qkv[...] = total[:, : 3 * width]
    grad_out[...] = total[:, 3 * width : 4 * width]
    grad_gain[...] = total[:, 4 * width :].T[:1, :]


def permuted(value, axis, target):
    count = lax.axis_size(axis)
    return lax.ppermute(value, axis, [(s, target(s) % count) for s in range(count)])


def all_to_all(value, axis, groups=None):
    return lax.all_to_all(
        value, axis, split_axis=0, concat_axis=0, tiled=True, axis_index_groups=groups
    )


def call(body, outs, scratch, args, flops, name, smem=False, space=58):
    shapes = [jax.ShapeDtypeStruct(s, d) for s, d in outs]
    return pl.pallas_call(
        body,
        out_shape=shapes,
        in_specs=[
            pl.BlockSpec(memory_space=pltpu.SMEM if smem and i == 0 else pltpu.VMEM)
            for i in range(len(args))
        ],
        out_specs=[pl.BlockSpec(memory_space=pltpu.VMEM)] * len(shapes),
        scratch_shapes=[pltpu.VMEM(s, d) for s, d in scratch],
        compiler_params=pltpu.CompilerParams(vmem_limit_bytes=space * 2**20),
        cost_estimate=pl.CostEstimate(flops=flops, bytes_accessed=2**21, transcendentals=0),
        name=name,
    )(*args)


def after(value, *others):
    return lax.optimization_barrier((value, *others))[0]


def on_device(feats, dest, anchor, ln_gain, w_qkv, w_out, cotangent):
    cells, width = feats.shape
    groups = lax.axis_size("grp")
    segments = lax.axis_size("seg")
    spill = cells // 16
    room = 2 * (cells - 2 * spill) // groups
    flat = groups * room
    early = 12
    row_i = ((1, cells), jnp.int32)
    rows_b = ((cells, width), bf16)
    turned = ((width, cells), bf16)
    heads_t = ((width + width // HEADS, cells), bf16)
    leg = ((flat, width), bf16)
    edge = ((spill, width), bf16)
    edges = ((spill, 2 * width), bf16)
    spots = ((cells, LANES), jnp.int32)
    zeroed = ((2, width, cells), bf16)
    tile_f = ((2, cells, PART), f32)
    tile_b = ((2, cells, PART), bf16)
    stat = ((5, 2, 8, PART), f32)
    acc = ((width // HEADS, cells), f32)
    work = [zeroed, zeroed, tile_f, tile_f, tile_f, tile_b, tile_b, stat, acc, acc]
    seg = lax.axis_index("seg").astype(jnp.int32)
    core = (seg % 2).reshape(1)
    gain = ln_gain.reshape(1, width)

    def exchange(rows):
        return all_to_all(rows.reshape(groups, room, -1), "grp").reshape(rows.shape)

    sizes = (segments, groups, room, spill)
    seg_ref = seg.reshape(1)
    home, x_out = call(
        lambda *refs: plan_kernel(*sizes, *refs), [row_i, leg], [],
        (seg_ref, dest.reshape(1, cells), feats), 2**32, "plan", smem=True,
    )
    x_in = exchange(x_out)
    take, g_out, up, down, w_t = call(
        lambda *refs: send_kernel(*sizes, *refs), [row_i, leg, edges, edges, ((3 * width, width), bf16)], [],
        (seg_ref, anchor.reshape(1, cells), home, feats, cotangent, w_qkv), 2**32, "send", smem=True,
    )
    low = permuted(up, "seg", lambda s: s + 1)
    high = permuted(down, "seg", lambda s: s - 1)
    g_in = exchange(after(g_out, x_in, low, high))
    xh, kv, q_t, k_t, v_t, ctx_t, lse = call(
        lambda *refs: forward_kernel(early, *refs),
        [rows_b, ((cells, 2 * width), bf16), turned, turned, turned, heads_t, ((HEADS * 8, cells), f32)],
        [spots, zeroed, tile_f, tile_f, tile_b, stat],
        (x_in, low, high, take, gain, w_qkv, w_t), 2**34, "forward",
    )
    half = width // 2
    wide = 4 * width + LANES
    halves = ((half, wide), f32)
    done, d_low, d_high, keep, give = call(
        lambda *refs: backward_kernel(early, *refs),
        [((flat, 2 * width), bf16), edges, edges, halves, halves],
        [
            spots, rows_b, turned, ((3 * width, cells), bf16), heads_t, heads_t, heads_t, heads_t,
            ((cells, 2 * width), bf16), ((width, wide), f32), *work,
        ],
        (core, g_in, low, high, take, xh, kv, q_t, k_t, v_t, ctx_t, lse, gain, w_t, w_out),
        2**36, "backward", smem=True,
    )
    done_in = exchange(done)
    above = permuted(d_low, "seg", lambda s: s - 1)
    below = permuted(d_high, "seg", lambda s: s + 1)

    depth = 4
    rows_x, rows_y = half // depth, half // depth**2
    other = lambda s: s + 1 - 2 * (s % 2)
    ahead_x = lambda k: lambda s: (s // 2 + k) % depth * 2 + s % 2
    ahead_y = lambda k: lambda g: g // depth * depth + (g % depth + k) % depth
    spot_x = (seg // 2).reshape(1)
    spot_y = (lax.axis_index("grp").astype(jnp.int32) % depth).reshape(1)

    def split(parts, spot, share):
        count = len(parts)
        own, *rest = call(
            lambda *refs: split_kernel(count, *refs),
            [((share, wide), f32)] * depth, [((share * depth, wide), f32)],
            (spot, *parts), 2**28, "split", smem=True, space=16,
        )
        return own, rest

    def join(parts, spot, share):
        return call(
            join_kernel, [((share * depth, wide), f32)], [], (spot, *parts), 2**28, "join", smem=True, space=16
        )[0]

    own, rest = split([keep, permuted(give, "seg", other)], spot_x, rows_x)
    rest = [permuted(part, "seg", ahead_x(k + 1)) for k, part in enumerate(rest)]
    own, rest = split([own, *rest], spot_y, rows_y)
    rest = [permuted(part, "grp", ahead_y(k + 1)) for k, part in enumerate(rest)]
    mine = call(
        lambda *refs: split_kernel(depth, *refs), [((rows_y, wide), f32)], [((rows_y, wide), f32)],
        (spot_y, own, *rest), 2**28, "sum", smem=True, space=16,
    )[0]
    layers = groups // depth
    ahead_z = lambda k: lambda g: (g // depth + k) % layers * depth + g % depth
    parts = [mine, *(permuted(mine, "grp", ahead_z(k)) for k in range(1, layers))]
    spot_z = (lax.axis_index("grp").astype(jnp.int32) // depth).reshape(1)
    mine = call(
        order_kernel, [((rows_y, wide), f32)], [((layers, rows_y, wide), f32)],
        (spot_z, *parts), 2**28, "order", smem=True, space=16,
    )[0]
    mine = after(mine, done_in, above, below)
    mine = join([mine, *(permuted(mine, "grp", ahead_y(k)) for k in range(1, depth))], spot_y, rows_y)
    mine = join([mine, *(permuted(mine, "seg", ahead_x(k)) for k in range(1, depth))], spot_x, rows_x)
    out_feats, grad_feats = (
        call(
            lambda *refs, side=side: home_kernel(side, *refs), [rows_b], [spots],
            (home, done_in, above, below), 2**32, "home",
        )[0]
        for side in range(2)
    )
    mine = after(mine, out_feats)
    theirs = permuted(mine, "seg", other)
    grad_qkv, grad_out, grad_gain = call(
        lambda *refs: finish_kernel((cells * segments * groups) ** -0.5, *refs),
        [((width, 3 * width), f32), ((width, width), f32), ((1, width), f32)],
        [((width, wide), f32)], (core, mine, theirs), 2**24, "finish", smem=True, space=16,
    )
    return out_feats, grad_feats, grad_qkv, grad_out, grad_gain.reshape(width)


def solution(mesh):
    split = P(("seg", "grp"), None)
    line = P(("seg", "grp"))
    return jax.shard_map(
        on_device,
        mesh=mesh,
        in_specs=(split, line, line, P(), P(), P(), split),
        out_specs=(split, split, P(), P(), P()),
        check_vma=False,
    )
```

```python
import jax
import jax.numpy as jnp
from jax import lax
from jax.experimental import pallas as pl
from jax.experimental.pallas import tpu as pltpu
from jax.sharding import PartitionSpec as P

HEADS = 16
LANES = 128
PART = 256
f32 = jnp.float32
bf16 = jnp.bfloat16


def nn(a, b):
    return lax.dot_general(a, b, (((1,), (0,)), ((), ())), preferred_element_type=f32)


def nt(a, b):
    return lax.dot_general(a, b, (((1,), (1,)), ((), ())), preferred_element_type=f32)


def tn(a, b):
    return lax.dot_general(a, b, (((0,), (0,)), ((), ())), preferred_element_type=f32)


def column_of(row):
    return jnp.broadcast_to(row, (8, row.shape[1])).T[:, :1]


def one_hot(mark, like):
    return jnp.where(mark == like, 1.0, 0.0).astype(bf16)


def slots_of(value, seg, segments, groups, room, spill):
    cells = value.shape[1]
    owner = lax.div(value, cells)
    owner_seg = lax.div(owner, groups)
    owner_grp = owner - owner_seg * groups
    first = lax.rem(seg + 1, segments)
    inside = owner_seg == seg
    is_first = owner_seg == first
    bucket = jnp.where(inside, owner_grp, jnp.where(is_first, groups, groups + 1))
    flat = groups * room
    base = jnp.where(inside, owner_grp * room, jnp.where(is_first, flat, flat + spill))
    return bucket, base


def ranks_of(bucket, order):
    cells = bucket.shape[1]
    bucket_col = column_of(bucket.astype(f32))
    order_col = column_of(order.astype(f32))
    bucket_row = bucket.astype(f32)
    order_row = order.astype(f32)
    total = jnp.zeros((8, cells), f32)
    for start in range(0, cells, 8):
        same = bucket_col[start : start + 8] == bucket_row
        ahead = order_col[start : start + 8] < order_row
        total = total + jnp.where(same & ahead, 1.0, 0.0)
    return jnp.sum(total, axis=0, keepdims=True).astype(jnp.int32)


def picks(spots, rows, flat, tail):
    mine = spots[rows, :1]
    main = one_hot(lax.broadcasted_iota(jnp.int32, (LANES, flat), 1), mine)
    rest = one_hot(lax.broadcasted_iota(jnp.int32, (LANES, tail), 1) + flat, mine)
    return main, rest


def spread_slots(slot_row, spots):
    spots[...] = jnp.broadcast_to(
        column_of(slot_row[...].astype(f32)).astype(jnp.int32), spots.shape
    )


def pool_pick(slot_row, arrived, first, second, spots, target):
    spread_slots(slot_row, spots)
    edge = jnp.concatenate([first, second], axis=0)
    for start in range(0, target.shape[0], LANES):
        rows = slice(start, start + LANES)
        main, rest = picks(spots, rows, arrived.shape[0], edge.shape[0])
        target[rows, :] = (nn(main, arrived[...]) + nn(rest, edge)).astype(bf16)


def rows_at(slot_row, rows, start, count):
    spots = lax.broadcasted_iota(jnp.int32, (count, rows.shape[0]), 0) + start
    return nn(one_hot(spots, slot_row[...]), rows[...]).astype(bf16)


def pool_place(slot_row, rows, out):
    for start in range(0, out.shape[0], PART):
        out[start : start + PART, :] = rows_at(slot_row, rows, start, PART)


def plan_kernel(segments, groups, room, spill, seg_ref, dest, feats, home, out):
    index = lax.broadcasted_iota(jnp.int32, dest.shape, 1)
    bucket, base = slots_of(dest[...], seg_ref[0], segments, groups, room, spill)
    home[...] = base + ranks_of(bucket, index)
    pool_place(home, feats, out)


def send_kernel(segments, groups, room, spill, seg_ref, anchor, home, feats, cot, w_qkv, take, out, up, down, w_t):
    width = feats.shape[1]
    flat = groups * room
    w_t[...] = w_qkv[...].astype(f32).T.astype(bf16)
    for rows, lanes in ((feats, slice(0, width)), (cot, slice(width, 2 * width))):
        tail = rows_at(home, rows, flat, 2 * spill)
        up[:, lanes] = tail[:spill]
        down[:, lanes] = tail[spill:]
    source = anchor[...]
    bucket, base = slots_of(source, seg_ref[0], segments, groups, room, spill)
    base = jnp.where(
        bucket == groups + 1, flat, jnp.where(bucket == groups, flat + spill, base)
    )
    take[...] = base + ranks_of(bucket, source)
    pool_place(home, cot, out)


def normalized(x, gain):
    xf = x.astype(f32)
    centered = xf - jnp.mean(xf, axis=-1, keepdims=True)
    rstd = lax.rsqrt(jnp.mean(centered * centered, axis=-1, keepdims=True) + 1e-05)
    xhat = centered * rstd
    return xhat, rstd, (xhat * gain).astype(bf16)


def attend(runs, k_all, v_all, refs, outs):
    q_t, k_t, v_t, d_t, q_zero, d_zero, score, expd, dprob, prob, dscore, stat, acc_v, acc_k = refs
    ctx_t, dq_t, dk_t, dv_t, lse = outs
    cells = score.shape[1]
    blocks = cells // PART
    size = q_t.shape[0] // HEADS
    TOP, SUM, INV, DOT, INNER = range(5)

    def rows(head):
        return pl.ds(pl.multiple_of(head * size, size), size)

    def rows8(head):
        return pl.ds(pl.multiple_of(head * 8, 8), 8)

    def part(index):
        return slice(index * PART, (index + 1) * PART)

    def fold(op, tile):
        return op(tile.reshape(PART // 8, 8, PART), axis=0)

    def combine(kind, block, piece, value, op):
        if piece:
            value = op(stat[kind, block % 2], value)
        stat[kind, block % 2] = value

    def spread(row):
        return jnp.broadcast_to(row, (8, PART))

    def set_head(mode, head):
        slot = lax.rem(head, 2)
        old = rows(lax.rem(head + HEADS - 2, HEADS))
        new = rows(head)
        q_zero[slot, old, :] = jnp.zeros((size, cells), bf16)
        q_zero[slot, new, :] = q_t[new, :]
        if mode != "forward":
            d_zero[slot, old, :] = jnp.zeros((size, cells), bf16)
            d_zero[slot, new, :] = d_t[new, :]

    def stage_scores(mode, head, block, piece):
        forward = mode != "backward"
        s = nn(k_all(part(piece)), q_zero[lax.rem(head, 2), :, part(block)])
        score[block % 2, part(piece), :] = s
        if forward:
            combine(TOP, block, piece, fold(jnp.max, s), jnp.maximum)
            if piece == blocks - 1:
                stat[TOP, block % 2] = spread(
                    jnp.max(stat[TOP, block % 2], axis=0, keepdims=True)
                )

    def stage_exp(mode, head, block, piece):
        forward, backward = mode != "backward", mode != "forward"
        slot = block % 2
        top = stat[TOP, slot][:1] if forward else lse[rows8(head), part(block)][:1]
        e = jnp.exp(score[slot, part(piece), :] - top)
        expd[slot, part(piece), :] = e
        if forward:
            combine(SUM, block, piece, fold(jnp.sum, e), jnp.add)
        if backward:
            dp = nn(v_all(part(piece)), d_zero[lax.rem(head, 2), :, part(block)])
            dprob[slot, part(piece), :] = dp
            combine(DOT, block, piece, fold(jnp.sum, e * dp), jnp.add)
        if piece == blocks - 1:
            if forward:
                total = jnp.sum(stat[SUM, slot], axis=0, keepdims=True)
                inverse = 1.0 / total
                stat[INV, slot] = spread(inverse)
                if mode == "forward":
                    lse[rows8(head), part(block)] = spread(top + jnp.log(total))
            if backward:
                inner = jnp.sum(stat[DOT, slot], axis=0, keepdims=True)
                stat[INNER, slot] = spread(inner * inverse if forward else inner)

    def stage_probs(mode, block, piece):
        forward, backward = mode != "backward", mode != "forward"
        slot = block % 2
        p = expd[slot, part(piece), :]
        if forward:
            p = p * stat[INV, slot][:1]
        prob[slot, part(piece), :] = p.astype(bf16)
        if backward:
            dp = dprob[slot, part(piece), :]
            dscore[slot, part(piece), :] = (p * (dp - stat[INNER, slot][:1])).astype(bf16)

    def stage_products(mode, head, spot, block, piece):
        forward, backward = mode != "backward", mode != "forward"
        mine, out, slot, cols = rows(head), rows(spot), block % 2, part(block)
        if forward and piece == 0:
            ctx_t[out, cols] = nn(v_t[mine, :], prob[slot]).astype(bf16)
        if backward:
            if piece == 1:
                dq_t[out, cols] = nn(k_t[mine, :], dscore[slot]).astype(bf16)
            if piece == 2:
                more = nt(d_t[mine, cols], prob[slot])
                acc_v[...] = more if block == 0 else acc_v[...] + more
            if piece == 3:
                more = nt(q_t[mine, cols], dscore[slot])
                acc_k[...] = more if block == 0 else acc_k[...] + more
                if block == blocks - 1:
                    dv_t[out, :] = acc_v[...].astype(bf16)
                    dk_t[out, :] = acc_k[...].astype(bf16)

    def body(mode, head, was, before, spot):
        for step in range(blocks if mode else blocks - 1):
            for piece in range(blocks):
                late = step - 3
                if late < 0:
                    stage_products(was, before, spot, late + blocks, piece)
                elif mode:
                    stage_products(mode, head, head, late, piece)
                if mode:
                    stage_scores(mode, head, step, piece)
                late = step - 2
                if late < 0:
                    stage_probs(was, late + blocks, piece)
                elif mode:
                    stage_probs(mode, late, piece)
                late = step - 1
                if late < 0:
                    stage_exp(was, before, late + blocks, piece)
                elif mode:
                    stage_exp(mode, head, late, piece)

    q_zero[...] = jnp.zeros_like(q_zero)
    if d_zero is not None:
        d_zero[...] = jnp.zeros_like(d_zero)
    was = before = None
    for mode, first, count in runs:
        start = first if was is None else first + 1
        if was is not None:
            set_head(mode, jnp.int32(first))
            body(mode, jnp.int32(first), was, jnp.int32(before), jnp.int32(before))

        def one_head(head, _, mode=mode, alone=None if was else first):
            set_head(mode, head)
            spot = head - 1 if alone is None else jnp.where(head == alone, HEADS, head - 1)
            body(mode, head, mode, lax.rem(head + HEADS - 1, HEADS), spot)
            return 0

        lax.fori_loop(start, first + count, one_head, 0)
        was, before = mode, first + count - 1
    body(None, None, was, jnp.int32(before), jnp.int32(before))


def forward_kernel(
    early, arrived, low, high, take, gain, w_qkv, w_t,
    xh, kv, q_t, k_t, v_t, ctx_t, lse,
    spots, *work,
):
    width = xh.shape[1]
    scale = (width // HEADS) ** -0.5
    pool_pick(take, arrived, low[:, :width], high[:, :width], spots, xh)
    _, _, normed = normalized(xh[...], gain[...])
    kv[...] = nn(normed, w_qkv[:, width:]).astype(bf16)
    q_t[...] = (nt(w_t[:width, :], normed).astype(bf16).astype(f32) * scale).astype(bf16)
    k_t[...] = (nt(w_t[width : 2 * width, :], normed).astype(bf16).astype(f32) * scale).astype(bf16)
    v_t[...] = nt(w_t[2 * width :, :], normed).astype(bf16)
    q_zero, score, expd, prob, stat = work
    refs = (q_t, k_t, v_t, None, q_zero, None, score, expd, None, prob, None, stat, None, None)
    attend(
        [("forward", 0, early)],
        lambda rows: kv[rows, :width], lambda rows: kv[rows, width:],
        refs, (ctx_t, None, None, None, lse),
    )


def backward_kernel(
    early, core, arrived, low, high, take, xh, kv, q_t, k_t, v_t, ctx_early, lse, gain, w_t, w_out,
    back, back_low, back_high, keep, give,
    spots, gh, d_t, d_qkv, ctx_t, dq_t, dk_t, dv_t, done, sums, *work,
):
    cells, width = xh.shape
    size = width // HEADS
    spill = back_low.shape[0]
    pool_pick(take, arrived, low[:, width:], high[:, width:], spots, gh)
    d_t[...] = nt(w_out[...], gh[...]).astype(bf16)
    q_zero, d_zero, score, expd, dprob, prob, dscore, stat, acc_v, acc_k = work
    refs = (q_t, k_t, v_t, d_t, q_zero, d_zero, score, expd, dprob, prob, dscore, stat, acc_v, acc_k)
    keys, values = lambda rows: kv[rows, :width], lambda rows: kv[rows, width:]
    attend(
        [("both", early, HEADS - early), ("backward", 0, early)],
        keys, values, refs, (ctx_t, dq_t, dk_t, dv_t, lse),
    )
    ctx_t[: early * size, :] = ctx_early[: early * size, :]
    for i, part in enumerate((dq_t, dk_t, dv_t)):
        d_qkv[i * width : (i + 1) * width, :] = part[:width, :]
    xhat, rstd, normed = normalized(xh[...], gain[...])
    dn = tn(d_qkv[...], w_t[...])
    part_gain = jnp.sum(dn * xhat, axis=0, keepdims=True)
    sums[:, : 3 * width] = nn(d_qkv[...], normed).T
    sums[:, 3 * width : 4 * width] = nn(ctx_t[:width, :], gh[...])
    sums[:, 4 * width :] = jnp.broadcast_to(part_gain, (LANES, width)).T
    half = width // 2
    mine = core[0]
    keep[...] = sums[pl.ds(pl.multiple_of(mine * half, half), half), :]
    give[...] = sums[pl.ds(pl.multiple_of((1 - mine) * half, half), half), :]
    dxhat = dn * gain[...]
    inner = (
        dxhat
        - jnp.mean(dxhat, axis=-1, keepdims=True)
        - xhat * jnp.mean(dxhat * xhat, axis=-1, keepdims=True)
    )
    done[:, :width] = (xh[...].astype(f32) + tn(ctx_t[:width, :], w_out[...])).astype(bf16)
    done[:, width:] = (gh[...].astype(f32) + inner * rstd).astype(bf16)
    pool_place(take, done, back)
    tail = rows_at(take, done, back.shape[0], 2 * spill)
    back_low[...] = tail[:spill]
    back_high[...] = tail[spill:]


def home_kernel(side, slot, arrived, first, second, out, spots):
    width = out.shape[1]
    lanes = slice(side * width, (side + 1) * width)
    pool_pick(slot, arrived.at[:, lanes], first[:, lanes], second[:, lanes], spots, out)


def split_kernel(count, spot, *refs):
    parts, outs, total = refs[:count], refs[count:-1], refs[-1]
    total[...] = sum(part[...] for part in parts[1:]) + parts[0][...]
    ways = len(outs)
    share = total.shape[0] // ways
    for k, out in enumerate(outs):
        start = lax.rem(spot[0] + k, ways) * share
        out[...] = total[pl.ds(pl.multiple_of(start, share), share), :]


def order_kernel(spot, *refs):
    parts, out, stack = refs[:-2], refs[-2], refs[-1]
    ways = len(parts)
    for k, part in enumerate(parts):
        stack[lax.rem(spot[0] + ways - k, ways)] = part[...]
    total = stack[0]
    for k in range(1, ways):
        total = total + stack[k]
    out[...] = total


def join_kernel(spot, *refs):
    parts, out = refs[:-1], refs[-1]
    ways = len(parts)
    share = parts[0].shape[0]
    for k, part in enumerate(parts):
        start = lax.rem(spot[0] + ways - k, ways) * share
        out[pl.ds(pl.multiple_of(start, share), share), :] = part[...]


def finish_kernel(factor, core, mine, other, grad_qkv, grad_out, grad_gain, total):
    width = grad_out.shape[1]
    half = mine.shape[0]
    total[pl.ds(pl.multiple_of(core[0] * half, half), half), :] = mine[...] * factor
    total[pl.ds(pl.multiple_of((1 - core[0]) * half, half), half), :] = other[...] * factor
    grad_qkv[...] = total[:, : 3 * width]
    grad_out[...] = total[:, 3 * width : 4 * width]
    grad_gain[...] = total[:, 4 * width :].T[:1, :]


def permuted(value, axis, target):
    count = lax.axis_size(axis)
    return lax.ppermute(value, axis, [(s, target(s) % count) for s in range(count)])


def all_to_all(value, axis, groups=None):
    return lax.all_to_all(
        value, axis, split_axis=0, concat_axis=0, tiled=True, axis_index_groups=groups
    )


def call(body, outs, scratch, args, flops, name, smem=False, space=58):
    shapes = [jax.ShapeDtypeStruct(s, d) for s, d in outs]
    return pl.pallas_call(
        body,
        out_shape=shapes,
        in_specs=[
            pl.BlockSpec(memory_space=pltpu.SMEM if smem and i == 0 else pltpu.VMEM)
            for i in range(len(args))
        ],
        out_specs=[pl.BlockSpec(memory_space=pltpu.VMEM)] * len(shapes),
        scratch_shapes=[pltpu.VMEM(s, d) for s, d in scratch],
        compiler_params=pltpu.CompilerParams(vmem_limit_bytes=space * 2**20),
        cost_estimate=pl.CostEstimate(flops=flops, bytes_accessed=2**21, transcendentals=0),
        name=name,
    )(*args)


def after(value, *others):
    return lax.optimization_barrier((value, *others))[0]


def on_device(feats, dest, anchor, ln_gain, w_qkv, w_out, cotangent):
    cells, width = feats.shape
    groups = lax.axis_size("grp")
    segments = lax.axis_size("seg")
    spill = cells // 16
    room = 2 * (cells - 2 * spill) // groups
    flat = groups * room
    early = 12
    row_i = ((1, cells), jnp.int32)
    rows_b = ((cells, width), bf16)
    turned = ((width, cells), bf16)
    heads_t = ((width + width // HEADS, cells), bf16)
    leg = ((flat, width), bf16)
    edge = ((spill, width), bf16)
    edges = ((spill, 2 * width), bf16)
    spots = ((cells, LANES), jnp.int32)
    zeroed = ((2, width, cells), bf16)
    tile_f = ((2, cells, PART), f32)
    tile_b = ((2, cells, PART), bf16)
    stat = ((5, 2, 8, PART), f32)
    acc = ((width // HEADS, cells), f32)
    work = [zeroed, zeroed, tile_f, tile_f, tile_f, tile_b, tile_b, stat, acc, acc]
    seg = lax.axis_index("seg").astype(jnp.int32)
    core = (seg % 2).reshape(1)
    gain = ln_gain.reshape(1, width)

    def exchange(rows):
        return all_to_all(rows.reshape(groups, room, -1), "grp").reshape(rows.shape)

    sizes = (segments, groups, room, spill)
    seg_ref = seg.reshape(1)
    home, x_out = call(
        lambda *refs: plan_kernel(*sizes, *refs), [row_i, leg], [],
        (seg_ref, dest.reshape(1, cells), feats), 2**32, "plan", smem=True,
    )
    x_in = exchange(x_out)
    take, g_out, up, down, w_t = call(
        lambda *refs: send_kernel(*sizes, *refs), [row_i, leg, edges, edges, ((3 * width, width), bf16)], [],
        (seg_ref, anchor.reshape(1, cells), home, feats, cotangent, w_qkv), 2**32, "send", smem=True,
    )
    low = permuted(up, "seg", lambda s: s + 1)
    high = permuted(down, "seg", lambda s: s - 1)
    g_in = exchange(after(g_out, x_in, low, high))
    xh, kv, q_t, k_t, v_t, ctx_t, lse = call(
        lambda *refs: forward_kernel(early, *refs),
        [rows_b, ((cells, 2 * width), bf16), turned, turned, turned, heads_t, ((HEADS * 8, cells), f32)],
        [spots, zeroed, tile_f, tile_f, tile_b, stat],
        (x_in, low, high, take, gain, w_qkv, w_t), 2**34, "forward",
    )
    half = width // 2
    wide = 4 * width + LANES
    halves = ((half, wide), f32)
    done, d_low, d_high, keep, give = call(
        lambda *refs: backward_kernel(early, *refs),
        [((flat, 2 * width), bf16), edges, edges, halves, halves],
        [
            spots, rows_b, turned, ((3 * width, cells), bf16), heads_t, heads_t, heads_t, heads_t,
            ((cells, 2 * width), bf16), ((width, wide), f32), *work,
        ],
        (core, g_in, low, high, take, xh, kv, q_t, k_t, v_t, ctx_t, lse, gain, w_t, w_out),
        2**36, "backward", smem=True,
    )
    done_in = exchange(done)
    above = permuted(d_low, "seg", lambda s: s - 1)
    below = permuted(d_high, "seg", lambda s: s + 1)

    depth = 4
    rows_x, rows_y = half // depth, half // depth**2
    other = lambda s: s + 1 - 2 * (s % 2)
    ahead_x = lambda k: lambda s: (s // 2 + k) % depth * 2 + s % 2
    ahead_y = lambda k: lambda g: g // depth * depth + (g % depth + k) % depth
    spot_x = (seg // 2).reshape(1)
    spot_y = (lax.axis_index("grp").astype(jnp.int32) % depth).reshape(1)

    def split(parts, spot, share):
        count = len(parts)
        own, *rest = call(
            lambda *refs: split_kernel(count, *refs),
            [((share, wide), f32)] * depth, [((share * depth, wide), f32)],
            (spot, *parts), 2**28, "split", smem=True, space=16,
        )
        return own, rest

    def join(parts, spot, share):
        return call(
            join_kernel, [((share * depth, wide), f32)], [], (spot, *parts), 2**28, "join", smem=True, space=16
        )[0]

    own, rest = split([keep, permuted(give, "seg", other)], spot_x, rows_x)
    rest = [permuted(part, "seg", ahead_x(k + 1)) for k, part in enumerate(rest)]
    own, rest = split([own, *rest], spot_y, rows_y)
    rest = [permuted(part, "grp", ahead_y(k + 1)) for k, part in enumerate(rest)]
    mine = call(
        lambda *refs: split_kernel(depth, *refs), [((rows_y, wide), f32)], [((rows_y, wide), f32)],
        (spot_y, own, *rest), 2**28, "sum", smem=True, space=16,
    )[0]
    ahead_z = lambda k: lambda g: g // depth**2 * depth**2 + (g + k * depth) % depth**2
    parts = [mine, *(permuted(mine, "grp", ahead_z(k)) for k in range(1, depth))]
    spot_z = (lax.axis_index("grp").astype(jnp.int32) // depth % depth).reshape(1)
    mine = call(
        order_kernel, [((rows_y, wide), f32)], [((depth, rows_y, wide), f32)],
        (spot_z, *parts), 2**28, "order", smem=True, space=16,
    )[0]
    step = depth**2
    while step < groups:
        mine = mine + permuted(mine, "grp", lambda g, step=step: g ^ step)
        step *= 2
    mine = after(mine, done_in, above, below)
    mine = join([mine, *(permuted(mine, "grp", ahead_y(k)) for k in range(1, depth))], spot_y, rows_y)
    mine = join([mine, *(permuted(mine, "seg", ahead_x(k)) for k in range(1, depth))], spot_x, rows_x)
    out_feats, grad_feats = (
        call(
            lambda *refs, side=side: home_kernel(side, *refs), [rows_b], [spots],
            (home, done_in, above, below), 2**32, "home",
        )[0]
        for side in range(2)
    )
    mine = after(mine, out_feats)
    theirs = permuted(mine, "seg", other)
    grad_qkv, grad_out, grad_gain = call(
        lambda *refs: finish_kernel((cells * segments * groups) ** -0.5, *refs),
        [((width, 3 * width), f32), ((width, width), f32), ((1, width), f32)],
        [((width, wide), f32)], (core, mine, theirs), 2**24, "finish", smem=True, space=16,
    )
    return out_feats, grad_feats, grad_qkv, grad_out, grad_gain.reshape(width)


def solution(mesh):
    split = P(("seg", "grp"), None)
    line = P(("seg", "grp"))
    return jax.shard_map(
        on_device,
        mesh=mesh,
        in_specs=(split, line, line, P(), P(), P(), split),
        out_specs=(split, split, P(), P(), P()),
        check_vma=False,
    )
```

```python
import jax
import jax.numpy as jnp
from jax import lax
from jax.experimental import pallas as pl
from jax.experimental.pallas import tpu as pltpu
from jax.sharding import PartitionSpec as P

HEADS = 16
LANES = 128
PART = 256
f32 = jnp.float32
bf16 = jnp.bfloat16


def nn(a, b):
    return lax.dot_general(a, b, (((1,), (0,)), ((), ())), preferred_element_type=f32)


def nt(a, b):
    return lax.dot_general(a, b, (((1,), (1,)), ((), ())), preferred_element_type=f32)


def tn(a, b):
    return lax.dot_general(a, b, (((0,), (0,)), ((), ())), preferred_element_type=f32)


def column_of(row):
    return jnp.broadcast_to(row, (8, row.shape[1])).T[:, :1]


def one_hot(mark, like):
    return jnp.where(mark == like, 1.0, 0.0).astype(bf16)


def slots_of(value, seg, segments, groups, room, spill):
    cells = value.shape[1]
    owner = lax.div(value, cells)
    owner_seg = lax.div(owner, groups)
    owner_grp = owner - owner_seg * groups
    first = lax.rem(seg + 1, segments)
    inside = owner_seg == seg
    is_first = owner_seg == first
    bucket = jnp.where(inside, owner_grp, jnp.where(is_first, groups, groups + 1))
    flat = groups * room
    base = jnp.where(inside, owner_grp * room, jnp.where(is_first, flat, flat + spill))
    return bucket, base


def ranks_of(bucket, order):
    cells = bucket.shape[1]
    bucket_col = column_of(bucket.astype(f32))
    order_col = column_of(order.astype(f32))
    bucket_row = bucket.astype(f32)
    order_row = order.astype(f32)
    total = jnp.zeros((8, cells), f32)
    for start in range(0, cells, 8):
        same = bucket_col[start : start + 8] == bucket_row
        ahead = order_col[start : start + 8] < order_row
        total = total + jnp.where(same & ahead, 1.0, 0.0)
    return jnp.sum(total, axis=0, keepdims=True).astype(jnp.int32)


def picks(spots, rows, flat, tail):
    mine = spots[rows, :1]
    main = one_hot(lax.broadcasted_iota(jnp.int32, (LANES, flat), 1), mine)
    rest = one_hot(lax.broadcasted_iota(jnp.int32, (LANES, tail), 1) + flat, mine)
    return main, rest


def spread_slots(slot_row, spots):
    spots[...] = jnp.broadcast_to(
        column_of(slot_row[...].astype(f32)).astype(jnp.int32), spots.shape
    )


def pool_pick(slot_row, arrived, first, second, spots, target):
    spread_slots(slot_row, spots)
    edge = jnp.concatenate([first, second], axis=0)
    for start in range(0, target.shape[0], LANES):
        rows = slice(start, start + LANES)
        main, rest = picks(spots, rows, arrived.shape[0], edge.shape[0])
        target[rows, :] = (nn(main, arrived[...]) + nn(rest, edge)).astype(bf16)


def rows_at(slot_row, rows, start, count):
    spots = lax.broadcasted_iota(jnp.int32, (count, rows.shape[0]), 0) + start
    return nn(one_hot(spots, slot_row[...]), rows[...]).astype(bf16)


def pool_place(slot_row, rows, out):
    for start in range(0, out.shape[0], PART):
        out[start : start + PART, :] = rows_at(slot_row, rows, start, PART)


def plan_kernel(segments, groups, room, spill, seg_ref, dest, feats, home, out):
    index = lax.broadcasted_iota(jnp.int32, dest.shape, 1)
    bucket, base = slots_of(dest[...], seg_ref[0], segments, groups, room, spill)
    home[...] = base + ranks_of(bucket, index)
    pool_place(home, feats, out)


def send_kernel(segments, groups, room, spill, seg_ref, anchor, home, feats, cot, w_qkv, take, out, up, down, w_t):
    width = feats.shape[1]
    flat = groups * room
    w_t[...] = w_qkv[...].astype(f32).T.astype(bf16)
    for rows, lanes in ((feats, slice(0, width)), (cot, slice(width, 2 * width))):
        tail = rows_at(home, rows, flat, 2 * spill)
        up[:, lanes] = tail[:spill]
        down[:, lanes] = tail[spill:]
    source = anchor[...]
    bucket, base = slots_of(source, seg_ref[0], segments, groups, room, spill)
    base = jnp.where(
        bucket == groups + 1, flat, jnp.where(bucket == groups, flat + spill, base)
    )
    take[...] = base + ranks_of(bucket, source)
    pool_place(home, cot, out)


def normalized(x, gain):
    xf = x.astype(f32)
    centered = xf - jnp.mean(xf, axis=-1, keepdims=True)
    rstd = lax.rsqrt(jnp.mean(centered * centered, axis=-1, keepdims=True) + 1e-05)
    xhat = centered * rstd
    return xhat, rstd, (xhat * gain).astype(bf16)


def attend(runs, k_all, v_all, refs, outs):
    q_t, k_t, v_t, d_t, q_zero, d_zero, score, expd, dprob, prob, dscore, stat, acc_v, acc_k = refs
    ctx_t, dq_t, dk_t, dv_t, lse = outs
    cells = score.shape[1]
    blocks = cells // PART
    size = q_t.shape[0] // HEADS
    TOP, SUM, INV, DOT, INNER = range(5)

    def rows(head):
        return pl.ds(pl.multiple_of(head * size, size), size)

    def rows8(head):
        return pl.ds(pl.multiple_of(head * 8, 8), 8)

    def part(index):
        return slice(index * PART, (index + 1) * PART)

    def fold(op, tile):
        return op(tile.reshape(PART // 8, 8, PART), axis=0)

    def combine(kind, block, piece, value, op):
        if piece:
            value = op(stat[kind, block % 2], value)
        stat[kind, block % 2] = value

    def spread(row):
        return jnp.broadcast_to(row, (8, PART))

    def set_head(mode, head):
        slot = lax.rem(head, 2)
        old = rows(lax.rem(head + HEADS - 2, HEADS))
        new = rows(head)
        q_zero[slot, old, :] = jnp.zeros((size, cells), bf16)
        q_zero[slot, new, :] = q_t[new, :]
        if mode != "forward":
            d_zero[slot, old, :] = jnp.zeros((size, cells), bf16)
            d_zero[slot, new, :] = d_t[new, :]

    def stage_scores(mode, head, block, piece):
        forward = mode != "backward"
        s = nn(k_all(part(piece)), q_zero[lax.rem(head, 2), :, part(block)])
        score[block % 2, part(piece), :] = s
        if forward:
            combine(TOP, block, piece, fold(jnp.max, s), jnp.maximum)
            if piece == blocks - 1:
                stat[TOP, block % 2] = spread(
                    jnp.max(stat[TOP, block % 2], axis=0, keepdims=True)
                )

    def stage_exp(mode, head, block, piece):
        forward, backward = mode != "backward", mode != "forward"
        slot = block % 2
        top = stat[TOP, slot][:1] if forward else lse[rows8(head), part(block)][:1]
        e = jnp.exp(score[slot, part(piece), :] - top)
        expd[slot, part(piece), :] = e
        if forward:
            combine(SUM, block, piece, fold(jnp.sum, e), jnp.add)
        if backward:
            dp = nn(v_all(part(piece)), d_zero[lax.rem(head, 2), :, part(block)])
            dprob[slot, part(piece), :] = dp
            combine(DOT, block, piece, fold(jnp.sum, e * dp), jnp.add)
        if piece == blocks - 1:
            if forward:
                total = jnp.sum(stat[SUM, slot], axis=0, keepdims=True)
                inverse = 1.0 / total
                stat[INV, slot] = spread(inverse)
                if mode == "forward":
                    lse[rows8(head), part(block)] = spread(top + jnp.log(total))
            if backward:
                inner = jnp.sum(stat[DOT, slot], axis=0, keepdims=True)
                stat[INNER, slot] = spread(inner * inverse if forward else inner)

    def stage_probs(mode, block, piece):
        forward, backward = mode != "backward", mode != "forward"
        slot = block % 2
        p = expd[slot, part(piece), :]
        if forward:
            p = p * stat[INV, slot][:1]
        prob[slot, part(piece), :] = p.astype(bf16)
        if backward:
            dp = dprob[slot, part(piece), :]
            dscore[slot, part(piece), :] = (p * (dp - stat[INNER, slot][:1])).astype(bf16)

    def stage_products(mode, head, spot, block, piece):
        forward, backward = mode != "backward", mode != "forward"
        mine, out, slot, cols = rows(head), rows(spot), block % 2, part(block)
        if forward and piece == 0:
            ctx_t[out, cols] = nn(v_t[mine, :], prob[slot]).astype(bf16)
        if backward:
            if piece == 1:
                dq_t[out, cols] = nn(k_t[mine, :], dscore[slot]).astype(bf16)
            if piece == 2:
                more = nt(d_t[mine, cols], prob[slot])
                acc_v[...] = more if block == 0 else acc_v[...] + more
            if piece == 3:
                more = nt(q_t[mine, cols], dscore[slot])
                acc_k[...] = more if block == 0 else acc_k[...] + more
                if block == blocks - 1:
                    dv_t[out, :] = acc_v[...].astype(bf16)
                    dk_t[out, :] = acc_k[...].astype(bf16)

    def body(mode, head, was, before, spot):
        for step in range(blocks if mode else blocks - 1):
            for piece in range(blocks):
                late = step - 3
                if late < 0:
                    stage_products(was, before, spot, late + blocks, piece)
                elif mode:
                    stage_products(mode, head, head, late, piece)
                if mode:
                    stage_scores(mode, head, step, piece)
                late = step - 2
                if late < 0:
                    stage_probs(was, late + blocks, piece)
                elif mode:
                    stage_probs(mode, late, piece)
                late = step - 1
                if late < 0:
                    stage_exp(was, before, late + blocks, piece)
                elif mode:
                    stage_exp(mode, head, late, piece)

    q_zero[...] = jnp.zeros_like(q_zero)
    if d_zero is not None:
        d_zero[...] = jnp.zeros_like(d_zero)
    was = before = None
    for mode, first, count in runs:
        start = first if was is None else first + 1
        if was is not None:
            set_head(mode, jnp.int32(first))
            body(mode, jnp.int32(first), was, jnp.int32(before), jnp.int32(before))

        def one_head(head, _, mode=mode, alone=None if was else first):
            set_head(mode, head)
            spot = head - 1 if alone is None else jnp.where(head == alone, HEADS, head - 1)
            body(mode, head, mode, lax.rem(head + HEADS - 1, HEADS), spot)
            return 0

        lax.fori_loop(start, first + count, one_head, 0)
        was, before = mode, first + count - 1
    body(None, None, was, jnp.int32(before), jnp.int32(before))


def forward_kernel(
    early, arrived, low, high, take, gain, w_qkv, w_t,
    xh, kv, q_t, k_t, v_t, ctx_t, lse,
    spots, *work,
):
    width = xh.shape[1]
    scale = (width // HEADS) ** -0.5
    pool_pick(take, arrived, low[:, :width], high[:, :width], spots, xh)
    _, _, normed = normalized(xh[...], gain[...])
    kv[...] = nn(normed, w_qkv[:, width:]).astype(bf16)
    q_t[...] = (nt(w_t[:width, :], normed).astype(bf16).astype(f32) * scale).astype(bf16)
    k_t[...] = (nt(w_t[width : 2 * width, :], normed).astype(bf16).astype(f32) * scale).astype(bf16)
    v_t[...] = nt(w_t[2 * width :, :], normed).astype(bf16)
    q_zero, score, expd, prob, stat = work
    refs = (q_t, k_t, v_t, None, q_zero, None, score, expd, None, prob, None, stat, None, None)
    attend(
        [("forward", 0, early)],
        lambda rows: kv[rows, :width], lambda rows: kv[rows, width:],
        refs, (ctx_t, None, None, None, lse),
    )


def backward_kernel(
    early, core, arrived, low, high, take, xh, kv, q_t, k_t, v_t, ctx_early, lse, gain, w_t, w_out,
    back, back_low, back_high, keep, give,
    spots, gh, d_t, d_qkv, ctx_t, dq_t, dk_t, dv_t, done, sums, *work,
):
    cells, width = xh.shape
    size = width // HEADS
    spill = back_low.shape[0]
    pool_pick(take, arrived, low[:, width:], high[:, width:], spots, gh)
    d_t[...] = nt(w_out[...], gh[...]).astype(bf16)
    q_zero, d_zero, score, expd, dprob, prob, dscore, stat, acc_v, acc_k = work
    refs = (q_t, k_t, v_t, d_t, q_zero, d_zero, score, expd, dprob, prob, dscore, stat, acc_v, acc_k)
    keys, values = lambda rows: kv[rows, :width], lambda rows: kv[rows, width:]
    attend(
        [("both", early, HEADS - early), ("backward", 0, early)],
        keys, values, refs, (ctx_t, dq_t, dk_t, dv_t, lse),
    )
    ctx_t[: early * size, :] = ctx_early[: early * size, :]
    for i, part in enumerate((dq_t, dk_t, dv_t)):
        d_qkv[i * width : (i + 1) * width, :] = part[:width, :]
    xhat, rstd, normed = normalized(xh[...], gain[...])
    dn = tn(d_qkv[...], w_t[...])
    part_gain = jnp.sum(dn * xhat, axis=0, keepdims=True)
    sums[:, : 3 * width] = nn(d_qkv[...], normed).T
    sums[:, 3 * width : 4 * width] = nn(ctx_t[:width, :], gh[...])
    sums[:, 4 * width :] = jnp.broadcast_to(part_gain, (LANES, width)).T
    half = width // 2
    mine = core[0]
    keep[...] = sums[pl.ds(pl.multiple_of(mine * half, half), half), :]
    give[...] = sums[pl.ds(pl.multiple_of((1 - mine) * half, half), half), :]
    dxhat = dn * gain[...]
    inner = (
        dxhat
        - jnp.mean(dxhat, axis=-1, keepdims=True)
        - xhat * jnp.mean(dxhat * xhat, axis=-1, keepdims=True)
    )
    done[:, :width] = (xh[...].astype(f32) + tn(ctx_t[:width, :], w_out[...])).astype(bf16)
    done[:, width:] = (gh[...].astype(f32) + inner * rstd).astype(bf16)
    pool_place(take, done, back)
    tail = rows_at(take, done, back.shape[0], 2 * spill)
    back_low[...] = tail[:spill]
    back_high[...] = tail[spill:]


def home_kernel(side, slot, arrived, first, second, out, spots):
    width = out.shape[1]
    lanes = slice(side * width, (side + 1) * width)
    pool_pick(slot, arrived.at[:, lanes], first[:, lanes], second[:, lanes], spots, out)


def split_kernel(count, spot, *refs):
    parts, outs, total = refs[:count], refs[count:-1], refs[-1]
    total[...] = sum(part[...] for part in parts[1:]) + parts[0][...]
    ways = len(outs)
    share = total.shape[0] // ways
    for k, out in enumerate(outs):
        start = lax.rem(spot[0] + k, ways) * share
        out[...] = total[pl.ds(pl.multiple_of(start, share), share), :]


def order_kernel(spot, *refs):
    parts, out, stack = refs[:-2], refs[-2], refs[-1]
    ways = len(parts)
    for k, part in enumerate(parts):
        stack[lax.rem(spot[0] + ways - k, ways)] = part[...]
    total = stack[0]
    for k in range(1, ways):
        total = total + stack[k]
    out[...] = total


def join_kernel(spot, *refs):
    parts, out = refs[:-1], refs[-1]
    ways = len(parts)
    share = parts[0].shape[0]
    for k, part in enumerate(parts):
        start = lax.rem(spot[0] + ways - k, ways) * share
        out[pl.ds(pl.multiple_of(start, share), share), :] = part[...]


def finish_kernel(factor, core, mine, other, grad_qkv, grad_out, grad_gain, total):
    width = grad_out.shape[1]
    half = mine.shape[0]
    total[pl.ds(pl.multiple_of(core[0] * half, half), half), :] = mine[...] * factor
    total[pl.ds(pl.multiple_of((1 - core[0]) * half, half), half), :] = other[...] * factor
    grad_qkv[...] = total[:, : 3 * width]
    grad_out[...] = total[:, 3 * width : 4 * width]
    grad_gain[...] = total[:, 4 * width :].T[:1, :]


def permuted(value, axis, target):
    count = lax.axis_size(axis)
    return lax.ppermute(value, axis, [(s, target(s) % count) for s in range(count)])


def all_to_all(value, axis, groups=None):
    return lax.all_to_all(
        value, axis, split_axis=0, concat_axis=0, tiled=True, axis_index_groups=groups
    )


def call(body, outs, scratch, args, flops, name, smem=False, space=58):
    shapes = [jax.ShapeDtypeStruct(s, d) for s, d in outs]
    return pl.pallas_call(
        body,
        out_shape=shapes,
        in_specs=[
            pl.BlockSpec(memory_space=pltpu.SMEM if smem and i == 0 else pltpu.VMEM)
            for i in range(len(args))
        ],
        out_specs=[pl.BlockSpec(memory_space=pltpu.VMEM)] * len(shapes),
        scratch_shapes=[pltpu.VMEM(s, d) for s, d in scratch],
        compiler_params=pltpu.CompilerParams(vmem_limit_bytes=space * 2**20),
        cost_estimate=pl.CostEstimate(flops=flops, bytes_accessed=2**21, transcendentals=0),
        name=name,
    )(*args)


def after(value, *others):
    return lax.optimization_barrier((value, *others))[0]


def on_device(feats, dest, anchor, ln_gain, w_qkv, w_out, cotangent):
    cells, width = feats.shape
    groups = lax.axis_size("grp")
    segments = lax.axis_size("seg")
    spill = cells // 16
    room = 2 * (cells - 2 * spill) // groups
    flat = groups * room
    early = 12
    row_i = ((1, cells), jnp.int32)
    rows_b = ((cells, width), bf16)
    turned = ((width, cells), bf16)
    heads_t = ((width + width // HEADS, cells), bf16)
    leg = ((flat, width), bf16)
    edge = ((spill, width), bf16)
    edges = ((spill, 2 * width), bf16)
    spots = ((cells, LANES), jnp.int32)
    zeroed = ((2, width, cells), bf16)
    tile_f = ((2, cells, PART), f32)
    tile_b = ((2, cells, PART), bf16)
    stat = ((5, 2, 8, PART), f32)
    acc = ((width // HEADS, cells), f32)
    work = [zeroed, zeroed, tile_f, tile_f, tile_f, tile_b, tile_b, stat, acc, acc]
    seg = lax.axis_index("seg").astype(jnp.int32)
    core = (seg % 2).reshape(1)
    gain = ln_gain.reshape(1, width)

    def exchange(rows):
        return all_to_all(rows.reshape(groups, room, -1), "grp").reshape(rows.shape)

    sizes = (segments, groups, room, spill)
    seg_ref = seg.reshape(1)
    home, x_out = call(
        lambda *refs: plan_kernel(*sizes, *refs), [row_i, leg], [],
        (seg_ref, dest.reshape(1, cells), feats), 2**32, "plan", smem=True,
    )
    x_in = exchange(x_out)
    take, g_out, up, down, w_t = call(
        lambda *refs: send_kernel(*sizes, *refs), [row_i, leg, edges, edges, ((3 * width, width), bf16)], [],
        (seg_ref, anchor.reshape(1, cells), home, feats, cotangent, w_qkv), 2**32, "send", smem=True,
    )
    low = permuted(up, "seg", lambda s: s + 1)
    high = permuted(down, "seg", lambda s: s - 1)
    g_in = exchange(after(g_out, x_in, low, high))
    xh, kv, q_t, k_t, v_t, ctx_t, lse = call(
        lambda *refs: forward_kernel(early, *refs),
        [rows_b, ((cells, 2 * width), bf16), turned, turned, turned, heads_t, ((HEADS * 8, cells), f32)],
        [spots, zeroed, tile_f, tile_f, tile_b, stat],
        (x_in, low, high, take, gain, w_qkv, w_t), 2**34, "forward",
    )
    half = width // 2
    wide = 4 * width + LANES
    halves = ((half, wide), f32)
    done, d_low, d_high, keep, give = call(
        lambda *refs: backward_kernel(early, *refs),
        [((flat, 2 * width), bf16), edges, edges, halves, halves],
        [
            spots, rows_b, turned, ((3 * width, cells), bf16), heads_t, heads_t, heads_t, heads_t,
            ((cells, 2 * width), bf16), ((width, wide), f32), *work,
        ],
        (core, g_in, low, high, take, xh, kv, q_t, k_t, v_t, ctx_t, lse, gain, w_t, w_out),
        2**36, "backward", smem=True,
    )
    done_in = exchange(done)
    above = permuted(d_low, "seg", lambda s: s - 1)
    below = permuted(d_high, "seg", lambda s: s + 1)

    depth = 4
    rows_x, rows_y = half // depth, half // depth**2
    other = lambda s: s + 1 - 2 * (s % 2)
    ahead_x = lambda k: lambda s: (s // 2 + k) % depth * 2 + s % 2
    ahead_y = lambda k: lambda g: g // depth * depth + (g % depth + k) % depth
    spot_x = (seg // 2).reshape(1)
    spot_y = (lax.axis_index("grp").astype(jnp.int32) % depth).reshape(1)

    def split(parts, spot, share):
        count = len(parts)
        own, *rest = call(
            lambda *refs: split_kernel(count, *refs),
            [((share, wide), f32)] * depth, [((share * depth, wide), f32)],
            (spot, *parts), 2**28, "split", smem=True, space=16,
        )
        return own, rest

    def join(parts, spot, share):
        return call(
            join_kernel, [((share * depth, wide), f32)], [], (spot, *parts), 2**28, "join", smem=True, space=16
        )[0]

    own, rest = split([keep, permuted(give, "seg", other)], spot_x, rows_x)
    rest = [permuted(part, "seg", ahead_x(k + 1)) for k, part in enumerate(rest)]
    own, rest = split([own, *rest], spot_y, rows_y)
    rest = [permuted(part, "grp", ahead_y(k + 1)) for k, part in enumerate(rest)]
    mine = call(
        lambda *refs: split_kernel(depth, *refs), [((rows_y, wide), f32)], [((rows_y, wide), f32)],
        (spot_y, own, *rest), 2**28, "sum", smem=True, space=16,
    )[0]
    ahead_z = lambda k: lambda g: g // depth**2 * depth**2 + (g + k * depth) % depth**2
    parts = [mine, *(permuted(mine, "grp", ahead_z(k)) for k in range(1, depth))]
    spot_z = (lax.axis_index("grp").astype(jnp.int32) // depth % depth).reshape(1)
    mine = call(
        order_kernel, [((rows_y, wide), f32)], [((depth, rows_y, wide), f32)],
        (spot_z, *parts), 2**28, "order", smem=True, space=16,
    )[0]
    step = depth**2
    while step < groups:
        mine = mine + permuted(mine, "grp", lambda g, step=step: g ^ step)
        step *= 2
    mine = after(mine, done_in, above, below)
    out_feats, grad_feats = (
        call(
            lambda *refs, side=side: home_kernel(side, *refs), [rows_b], [spots],
            (home, done_in, above, below), 2**32, "home",
        )[0]
        for side in range(2)
    )
    mine = join([mine, *(permuted(mine, "grp", ahead_y(k)) for k in range(1, depth))], spot_y, rows_y)
    mine = after(mine, out_feats)
    mine = join([mine, *(permuted(mine, "seg", ahead_x(k)) for k in range(1, depth))], spot_x, rows_x)
    mine = after(mine, grad_feats)
    theirs = permuted(mine, "seg", other)
    grad_qkv, grad_out, grad_gain = call(
        lambda *refs: finish_kernel((cells * segments * groups) ** -0.5, *refs),
        [((width, 3 * width), f32), ((width, width), f32), ((1, width), f32)],
        [((width, wide), f32)], (core, mine, theirs), 2**24, "finish", smem=True, space=16,
    )
    return out_feats, grad_feats, grad_qkv, grad_out, grad_gain.reshape(width)


def solution(mesh):
    split = P(("seg", "grp"), None)
    line = P(("seg", "grp"))
    return jax.shard_map(
        on_device,
        mesh=mesh,
        in_specs=(split, line, line, P(), P(), P(), split),
        out_specs=(split, split, P(), P(), P()),
        check_vma=False,
    )
```
